512 devices in a mesh: pts: 512 (over x, y, z, core).
Axes of the slice: x: 4, y: 8, z: 8, core: 2. Of those that a mesh axis runs over, the one named last changes fastest.
Arguments:
- coords: int32 [2, 262144], P(None, 'pts'), may hold values from 0 to 262143, as said below
- probes: int32 [16, 262144], P(None, 'pts'), may hold values from 0 to 1
- u_bases: bfloat16 [1600, 262144], P(None, 'pts')
- v_bases: bfloat16 [1600, 262144], P(None, 'pts')
Outputs:
- forward: float32 [16, 262144], P(None, 'pts')
- transposed: float32 [16, 262144], P(None, 'pts')
The draws below stay inside these ranges and needn't reach their ends.
Inputs may be any that keep to these rules, and one draw needn't show every extreme that they name: `coords`: points are laid leaf by leaf; leaf k's point i sits in grid cell (k * 16 + i % 16, i // 16); each component is 16 times its cell index plus a jitter of 0 to 15; the first point's jitter is 0 and the last point's is 15.
All inputs are finite; a program needn't handle non-finite values.
Results may differ from the reference program's by a relative error of at most 0.0028.
Values may be sent and summed in bfloat16 or wider, within the bound.
A program may use at most 64 MiB of HBM per device.

```python
import math
import jax
import jax.numpy as jnp
import numpy as np
from jax import lax

SIDE = 16
LEAF = 256
P_DEV = 512
RANK_UNIT = 64
NPROBE = 16
RSUM = 1600
POINTS = 262144
N_PTS = 512


jitter_cells = 16


factor_list = (1, 1, 1, 1, 2, 2, 4, 4, 8, 8)


def scale_table(for_left):
    level_bits = N_PTS.bit_length() - 1
    first = RANK_UNIT if for_left else LEAF
    scale_list = [1.0 / math.sqrt(first)] * RANK_UNIT
    for level in range(level_bits):
        width = RANK_UNIT * factor_list[level]
        count = width if for_left else P_DEV * 2 ** level
        scale_list = scale_list + [1.0 / math.sqrt(count)] * width
    return np.array(scale_list, dtype=np.float32)


def draw_coords(key, part):
    key = jax.random.fold_in(key, 11)
    index = jnp.arange(POINTS, dtype=jnp.int32)
    leaf_index = index // LEAF
    within = index % LEAF
    cell_x = leaf_index * SIDE + within % SIDE
    cell_y = within // SIDE
    jitter = jax.random.randint(key, (2, POINTS), 0, jitter_cells, dtype=jnp.int32)
    position = jnp.arange(POINTS, dtype=jnp.int32)[None, :]
    jitter = jnp.where(position == 0, 0, jitter)
    jitter = jnp.where(position == POINTS - 1, jitter_cells - 1, jitter)
    return jnp.stack([cell_x, cell_y]) * jitter_cells + jitter


def draw_u_bases(key, part):
    key = jax.random.fold_in(key, 5)
    normal_key, spread_key = jax.random.split(key)
    values = jax.random.normal(normal_key, (RSUM, POINTS), jnp.float32)
    return (values * jnp.asarray(scale_table(True))[:, None]).astype(jnp.bfloat16)


def draw_v_bases(key, part):
    key = jax.random.fold_in(key, 7)
    normal_key, spread_key = jax.random.split(key)
    values = jax.random.normal(normal_key, (RSUM, POINTS), jnp.float32)
    return (values * jnp.asarray(scale_table(False))[:, None]).astype(jnp.bfloat16)


def set_ends(values, rng, smallest, top_value):
    extent = values.shape
    index_at = [jax.random.randint(jax.random.fold_in(rng, axis), (), 0, extent[axis]) for axis in range(len(extent))]
    values = values.at[tuple(index_at)].set(smallest)
    longest = extent.index(max(extent))
    index_at[longest] = (index_at[longest] + 1) % extent[longest]
    return values.at[tuple(index_at)].set(top_value)


def setup_inputs(seed: int = 0) -> dict:
    key_list = jax.random.split(jax.random.key(seed), 5)
    return {
        "coords": draw_coords(jax.random.fold_in(key_list[4], 71), 0),
        "probes": set_ends(jax.random.randint(key_list[1], (NPROBE, POINTS), 0, 2), jax.random.fold_in(key_list[1], 1), 0, 1).astype(jnp.int32),
        "u_bases": draw_u_bases(jax.random.fold_in(key_list[4], 71), 0),
        "v_bases": draw_v_bases(jax.random.fold_in(key_list[4], 71), 0),
    }


factor_list = (1, 1, 1, 1, 2, 2, 4, 4, 8, 8)
cell_units = 16.0
length_scale = 4.0
root_three = 1.7320508075688772
nugget = 0.1

def matern_leaf(points):
    spots = points.astype(jnp.float32) / cell_units
    delta_x = spots[0][:, None] - spots[0][None, :]
    delta_y = spots[1][:, None] - spots[1][None, :]
    scaled = root_three * jnp.sqrt(delta_x * delta_x + delta_y * delta_y) / length_scale
    kernel = (1.0 + scaled) * jnp.exp(-scaled) + nugget * jnp.eye(points.shape[1], dtype=jnp.float32)
    return kernel.astype(jnp.bfloat16)

def level_term(sign_rows, contract_rows, apply_rows, node):
    width = contract_rows.shape[0]
    pairs = POINTS // node // 2
    signs_split = sign_rows.reshape(NPROBE, pairs, 2, node)
    contract_split = contract_rows.astype(jnp.float32).reshape(width, pairs, 2, node)
    coef = jnp.einsum('pmsn,rmsn->pmsr', signs_split, contract_split, precision=lax.Precision.HIGHEST)
    sibling = lax.optimization_barrier(jnp.flip(coef, axis=2).astype(jnp.bfloat16))
    sibling = sibling.astype(jnp.float32)
    apply_split = apply_rows.astype(jnp.float32).reshape(width, pairs, 2, node)
    result = jnp.einsum('pmsr,rmsn->pmsn', sibling, apply_split, precision=lax.Precision.HIGHEST)
    return result.reshape(NPROBE, POINTS)

def reference(coords, probes, u_bases, v_bases):
    sign_rows = (2 * probes - 1).astype(jnp.float32)
    leaf_count = POINTS // LEAF
    leaf_points = coords.reshape(2, leaf_count, LEAF).transpose(1, 0, 2)
    leaf_signs = sign_rows.reshape(NPROBE, leaf_count, LEAF).transpose(1, 0, 2)

    def one_leaf(item):
        points, signs = item
        block = matern_leaf(points).astype(jnp.float32)
        return jnp.dot(signs, block, precision=lax.Precision.HIGHEST)
    near = lax.map(one_leaf, (leaf_points, leaf_signs))
    near = near.transpose(1, 0, 2).reshape(NPROBE, POINTS)
    level_bits = N_PTS.bit_length() - 1
    levels = [(0, RANK_UNIT, LEAF)]
    start = RANK_UNIT
    for level in range(level_bits):
        width = RANK_UNIT * factor_list[level]
        levels.append((start, width, P_DEV * 2 ** level))
        start = start + width
    forward = near
    transposed = near
    for first, width, node in levels:
        u_rows = u_bases[first:first + width]
        v_rows = v_bases[first:first + width]
        forward = forward + level_term(sign_rows, v_rows, u_rows, node)
        transposed = transposed + level_term(sign_rows, u_rows, v_rows, node)
    return (forward, transposed)
```

```python
import jax
import jax.numpy as jnp
from jax import lax
from jax.experimental import pallas as pl
from jax.experimental.pallas import tpu as pltpu
from jax.sharding import PartitionSpec as P

MESH = pl.DeviceIdType.MESH
F32 = jnp.float32
BF16 = jnp.bfloat16

LEAF = 256
POINTS_HERE = 512
RANKS = 1600
LOW, MID, TOP7, TOP8 = 0, 320, 832, 1088

cell_units = 16.0
length_scale = 4.0
root_three = 1.7320508075688772
nugget = 0.1


def device(x, y, z, c):
    return ((x * 8 + y) * 8 + z) * 2 + c


def nt(a, b):
    return lax.dot_general(a, b, (((1,), (1,)), ((), ())), preferred_element_type=F32)


def nn(a, b):
    return jnp.dot(a, b, preferred_element_type=F32)


def send(src, dst, send_sem, recv_sem, to):
    pltpu.make_async_remote_copy(
        src_ref=src,
        dst_ref=dst,
        send_sem=send_sem,
        recv_sem=recv_sem,
        device_id=(to,),
        device_id_type=MESH,
    ).start()


def wait(ref, sem):
    pltpu.make_async_copy(ref, ref, sem).wait()


def matern(spots, leaf):
    cols = spots[:, leaf * LEAF : (leaf + 1) * LEAF]
    tall = jnp.transpose(cols)
    delta_x = tall[:, 0:1] - cols[0:1, :]
    delta_y = tall[:, 1:2] - cols[1:2, :]
    scaled = (root_three / length_scale) * jnp.sqrt(delta_x * delta_x + delta_y * delta_y)
    row = lax.broadcasted_iota(jnp.int32, (LEAF, LEAF), 0)
    col = lax.broadcasted_iota(jnp.int32, (LEAF, LEAF), 1)
    block = (1.0 + scaled) * jnp.exp(-scaled) + jnp.where(row == col, nugget, 0.0)
    return block.astype(BF16)


def kernel(
    coords_hbm, probes_hbm, u_hbm, v_hbm, f_ref, t_ref,
    coords, probes, signs, u, v,
    snd, low_snd, low0,
    r8, r7, r4, p8, p7, p4, q8, q7, q4, q1, q2, q3, fin,
    load, s1, s2, s3, sl, rs,
):
    me = lax.axis_index("pts")
    c = me % 2
    z = (me // 2) % 8
    y = (me // 16) % 8
    x = me // 128
    yc = y * 2 + c
    zc = z * 2 + c
    core0 = c == 0
    core1 = c == 1
    owner7 = jnp.logical_and(core1, y % 2 == 0)

    loads = [
        (probes_hbm, probes, None),
        (v_hbm, v, (TOP8, 512)),
        (u_hbm, u, (TOP8, 512)),
        (v_hbm, v, (TOP7, 256)),
        (u_hbm, u, (TOP7, 256)),
        (v_hbm, v, (MID, 512)),
        (u_hbm, u, (MID, 512)),
        (v_hbm, v, (LOW, 320)),
        (u_hbm, u, (LOW, 320)),
        (coords_hbm, coords, None),
    ]
    copies = []
    for i, (src, dst, rows) in enumerate(loads):
        if rows is not None:
            src, dst = src.at[pl.ds(*rows)], dst.at[pl.ds(*rows)]
        copies.append(pltpu.make_async_copy(src, dst, load.at[i]))
        copies[-1].start()

    barrier = pltpu.get_barrier_semaphore()

    def greet(to):
        pl.semaphore_signal(barrier, inc=1, device_id=(to,), device_id_type=MESH)

    @pl.loop(1, 16)
    def _(j):
        o = (yc + j) % 16
        greet(device(x, o // 2, z, o % 2))
        o = (zc + j) % 16
        greet(device(x, y, o // 2, o % 2))

    half = 2 - (x // 2) * 2
    beside = x + 1 - 2 * (x % 2)

    @pl.when(core0)
    def _():
        @pl.loop(0, 16)
        def _(j):
            greet(device(half + j // 8, y, j % 8, 0))

    @pl.when(core1)
    def _():
        @pl.loop(0, 8)
        def _(j):
            greet(device(beside, y, j, 1))

    copies[0].wait()
    signs[...] = (2 * probes[...] - 1).astype(BF16)

    copies[1].wait()
    part = nt(signs[...], v[pl.ds(TOP8, 512), :])
    for k in range(4):
        snd[k] = part[:, k * 128 : (k + 1) * 128]
    copies[2].wait()
    part = nt(signs[...], u[pl.ds(TOP8, 512), :])
    for k in range(4):
        snd[4 + k] = part[:, k * 128 : (k + 1) * 128]

    @pl.when(core0)
    def _():
        pl.semaphore_wait(barrier, 46)

    @pl.when(core1)
    def _():
        pl.semaphore_wait(barrier, 38)

    @pl.loop(1, 8)
    def _(j):
        k = (y + j) % 8
        send(snd.at[k], r8.at[yc], s1.at[0], rs.at[0], device(x, k, z, 0))

    @pl.when(core1)
    def _():
        send(snd.at[y], r8.at[yc], s1.at[1], rs.at[0], device(x, y, z, 0))

    @pl.when(core0)
    def _():
        r8[yc] = snd[y]

    copies[3].wait()
    part = nt(signs[...], v[pl.ds(TOP7, 256), :])
    for k in range(2):
        snd[8 + k] = part[:, k * 128 : (k + 1) * 128]
    copies[4].wait()
    part = nt(signs[...], u[pl.ds(TOP7, 256), :])
    for k in range(2):
        snd[10 + k] = part[:, k * 128 : (k + 1) * 128]

    @pl.loop(1, 4)
    def _(j):
        k = (y // 2 + j) % 4
        send(snd.at[8 + k], r7.at[yc], s1.at[2], rs.at[1], device(x, 2 * k, z, 1))

    @pl.when(jnp.logical_not(owner7))
    def _():
        k = y // 2
        send(snd.at[8 + k], r7.at[yc], s1.at[3], rs.at[1], device(x, 2 * k, z, 1))

    @pl.when(owner7)
    def _():
        r7[yc] = snd[8 + y // 2]

    copies[5].wait()
    part = nt(signs[...], v[pl.ds(MID, 512), :])
    for k, to in enumerate((0, 2, 4, 5)):
        snd[12 + to] = part[:, k * 128 : (k + 1) * 128]
    copies[6].wait()
    part = nt(signs[...], u[pl.ds(MID, 512), :])
    for k, to in enumerate((1, 3, 6, 7)):
        snd[12 + to] = part[:, k * 128 : (k + 1) * 128]

    @pl.loop(1, 8)
    def _(j):
        k = (z + j) % 8
        send(snd.at[12 + k], r4.at[zc], s1.at[4], rs.at[2], device(x, y, k, 1))

    @pl.when(core0)
    def _():
        send(snd.at[12 + z], r4.at[zc], s1.at[5], rs.at[2], device(x, y, z, 1))

    @pl.when(core1)
    def _():
        r4[zc] = snd[12 + z]

    copies[7].wait()
    low_f = nt(signs[...], v[pl.ds(64, 256), :])
    copies[8].wait()
    low_t = nt(signs[...], u[pl.ds(64, 256), :])
    joined = [
        jnp.concatenate([low_f[:, k * 64 : (k + 1) * 64], low_t[:, k * 64 : (k + 1) * 64]], axis=1)
        for k in range(4)
    ]
    low0[...] = joined[0].astype(BF16)
    for k in range(3):
        low_snd[k] = joined[k + 1]
    send(low0, fin.at[20], sl.at[0], rs.at[3], device(x, y, z, 1 - c))
    chip1 = z + 1 - 2 * (z % 2)
    send(low_snd.at[0], q1.at[c], sl.at[1], rs.at[4], device(x, y, chip1, 0))
    send(low_snd.at[0], q1.at[c], sl.at[2], rs.at[4], device(x, y, chip1, 1))
    pair = z // 2
    sib_pair = pair + 1 - 2 * (pair % 2)
    send(low_snd.at[1], q2.at[zc % 4], sl.at[3], rs.at[5], device(x, y, 2 * sib_pair + 1, 0))
    quad = z // 4
    send(low_snd.at[2], q3.at[zc % 8], sl.at[4], rs.at[6], device(x, y, 4 * (1 - quad) + 2, 0))

    @pl.when(core0)
    def _():
        wait(r8.at[pl.ds(0, 15)], rs.at[0])
        p8[...] = jnp.sum(r8[...], axis=0)

        @pl.loop(0, 16)
        def _(j):
            send(p8, q8.at[(x % 2) * 8 + z], s2.at[0], rs.at[7], device(half + j // 8, y, j % 8, 0))

    @pl.when(owner7)
    def _():
        wait(r7.at[pl.ds(0, 15)], rs.at[1])
        p7[...] = jnp.sum(r7[...], axis=0)

        @pl.loop(0, 8)
        def _(j):
            send(p7, q7.at[z], s2.at[1], rs.at[8], device(beside, y, j, 1))

    def mid_levels(action):
        for n, chosen in ((1, z < 2), (2, jnp.logical_and(z >= 2, z < 4)), (4, z >= 4)):
            @pl.when(jnp.logical_and(core1, chosen))
            def _():
                action(n)

    @pl.when(core1)
    def _():
        wait(r4.at[pl.ds(0, 15)], rs.at[2])
        p4[...] = jnp.sum(r4[...], axis=0)

    def mid_send(n):
        node = y // n
        first = (node + 1 - 2 * (node % 2)) * n
        for j in range(n):
            send(p4, q4.at[y % n], s2.at[2], rs.at[9], device(x, first + j, z, 1))

    mid_levels(mid_send)

    copies[9].wait()
    spots = coords[...].astype(F32) / cell_units
    for leaf in range(2):
        cols = pl.ds(leaf * LEAF, LEAF)
        other = pl.ds((1 - leaf) * LEAF, LEAF)
        near = nn(signs[:, cols], matern(spots, leaf))
        coef_f = nt(signs[:, other], v[pl.ds(0, 64), other]).astype(BF16)
        coef_t = nt(signs[:, other], u[pl.ds(0, 64), other]).astype(BF16)
        f_ref[:, cols] = near + nn(coef_f, u[pl.ds(0, 64), cols])
        t_ref[:, cols] = near + nn(coef_t, v[pl.ds(0, 64), cols])

    owner2 = jnp.logical_and(core0, z % 2 == 1)
    owner3 = jnp.logical_and(core0, z % 4 == 2)

    @pl.when(owner2)
    def _():
        wait(q2, rs.at[5])
        fin[22] = jnp.sum(q2[...], axis=0).astype(BF16)
        for j in range(1, 4):
            o = (zc % 4 + j) % 4
            send(fin.at[22], fin.at[22], s3.at[0], rs.at[10], device(x, y, 2 * pair + o // 2, o % 2))

    @pl.when(owner3)
    def _():
        wait(q3, rs.at[6])
        fin[23] = jnp.sum(q3[...], axis=0).astype(BF16)
        for j in range(1, 8):
            o = (zc % 8 + j) % 8
            send(fin.at[23], fin.at[23], s3.at[1], rs.at[11], device(x, y, 4 * quad + o // 2, o % 2))

    def mid_sum(n):
        wait(q4.at[pl.ds(0, n)], rs.at[9])
        fin[12 + z] = jnp.sum(q4[pl.ds(0, n)], axis=0).astype(BF16)

        @pl.loop(1, 16)
        def _(j):
            o = (zc + j) % 16
            send(fin.at[12 + z], fin.at[12 + z], s3.at[2], rs.at[12], device(x, y, o // 2, o % 2))

    mid_levels(mid_sum)

    @pl.when(core0)
    def _():
        wait(q8, rs.at[7])
        fin[y] = jnp.sum(q8[...], axis=0).astype(BF16)

        @pl.loop(1, 16)
        def _(j):
            o = (yc + j) % 16
            send(fin.at[y], fin.at[y], s3.at[3], rs.at[13], device(x, o // 2, z, o % 2))

    @pl.when(owner7)
    def _():
        wait(q7, rs.at[8])
        fin[8 + y // 2] = jnp.sum(q7[...], axis=0).astype(BF16)

        @pl.loop(1, 16)
        def _(j):
            o = (yc + j) % 16
            send(
                fin.at[8 + y // 2], fin.at[8 + y // 2], s3.at[4], rs.at[14], device(x, o // 2, z, o % 2)
            )

    wait(low0, rs.at[3])
    wait(q1, rs.at[4])
    fin[21] = jnp.sum(q1[...], axis=0).astype(BF16)

    @pl.when(jnp.logical_not(owner2))
    def _():
        wait(low0, rs.at[10])

    @pl.when(jnp.logical_not(owner3))
    def _():
        wait(low0, rs.at[11])

    low = [fin[20 + k] for k in range(4)]
    low_f = jnp.concatenate([part[:, :64] for part in low], axis=1)
    low_t = jnp.concatenate([part[:, 64:] for part in low], axis=1)
    f_ref[...] += nn(low_f, u[pl.ds(64, 256), :])
    t_ref[...] += nn(low_t, v[pl.ds(64, 256), :])

    @pl.when(core0)
    def _():
        wait(fin.at[pl.ds(0, 8)], rs.at[12])

    @pl.when(core1)
    def _():
        wait(fin.at[pl.ds(0, 7)], rs.at[12])

    def joint(chunks):
        return jnp.concatenate([fin[k] for k in chunks], axis=1)

    f_ref[...] += nn(joint((12, 14, 16, 17)), u[pl.ds(MID, 512), :])
    t_ref[...] += nn(joint((13, 15, 18, 19)), v[pl.ds(MID, 512), :])

    @pl.when(owner7)
    def _():
        wait(fin.at[pl.ds(0, 3)], rs.at[14])

    @pl.when(jnp.logical_not(owner7))
    def _():
        wait(fin.at[pl.ds(0, 4)], rs.at[14])

    @pl.when(core0)
    def _():
        wait(fin.at[pl.ds(0, 7)], rs.at[13])

    @pl.when(core1)
    def _():
        wait(fin.at[pl.ds(0, 8)], rs.at[13])

    f_ref[...] += nn(joint((8, 9, 0, 1, 2, 3)), u[pl.ds(TOP7, 768), :])
    t_ref[...] += nn(joint((10, 11, 4, 5, 6, 7)), v[pl.ds(TOP7, 768), :])

    wait(r8.at[pl.ds(0, 7)], s1.at[0])
    wait(r8.at[pl.ds(0, 3)], s1.at[2])
    wait(r8.at[pl.ds(0, 7)], s1.at[4])

    @pl.when(jnp.logical_not(owner7))
    def _():
        wait(p7, s1.at[3])

    wait(low0, sl.at[0])
    for k in range(1, 5):
        wait(p7, sl.at[k])

    @pl.when(core0)
    def _():
        wait(p4, s1.at[5])
        wait(q8, s2.at[0])
        wait(fin.at[pl.ds(0, 15)], s3.at[3])

    @pl.when(core1)
    def _():
        wait(p8, s1.at[1])
        wait(fin.at[pl.ds(0, 15)], s3.at[2])

    @pl.when(owner7)
    def _():
        wait(q7, s2.at[1])
        wait(fin.at[pl.ds(0, 15)], s3.at[4])

    mid_levels(lambda n: wait(q4.at[pl.ds(0, n)], s2.at[2]))

    @pl.when(owner2)
    def _():
        wait(fin.at[pl.ds(0, 3)], s3.at[0])

    @pl.when(owner3)
    def _():
        wait(fin.at[pl.ds(0, 7)], s3.at[1])


def shards(coords, probes, u_bases, v_bases):
    tile = (16, 128)
    return pl.pallas_call(
        kernel,
        out_shape=[jax.ShapeDtypeStruct((16, POINTS_HERE), F32)] * 2,
        in_specs=[pl.BlockSpec(memory_space=pl.ANY)] * 4,
        out_specs=[pl.BlockSpec(memory_space=pltpu.VMEM)] * 2,
        scratch_shapes=[
            pltpu.VMEM((2, POINTS_HERE), jnp.int32),
            pltpu.VMEM((16, POINTS_HERE), jnp.int32),
            pltpu.VMEM((16, POINTS_HERE), BF16),
            pltpu.VMEM((RANKS, POINTS_HERE), BF16),
            pltpu.VMEM((RANKS, POINTS_HERE), BF16),
            pltpu.VMEM((20,) + tile, F32),
            pltpu.VMEM((3,) + tile, F32),
            pltpu.VMEM(tile, BF16),
            pltpu.VMEM((16,) + tile, F32),
            pltpu.VMEM((16,) + tile, F32),
            pltpu.VMEM((16,) + tile, F32),
            pltpu.VMEM(tile, F32),
            pltpu.VMEM(tile, F32),
            pltpu.VMEM(tile, F32),
            pltpu.VMEM((16,) + tile, F32),
            pltpu.VMEM((8,) + tile, F32),
            pltpu.VMEM((4,) + tile, F32),
            pltpu.VMEM((2,) + tile, F32),
            pltpu.VMEM((4,) + tile, F32),
            pltpu.VMEM((8,) + tile, F32),
            pltpu.VMEM((24,) + tile, BF16),
            pltpu.SemaphoreType.DMA((10,)),
            pltpu.SemaphoreType.DMA((6,)),
            pltpu.SemaphoreType.DMA((3,)),
            pltpu.SemaphoreType.DMA((5,)),
            pltpu.SemaphoreType.DMA((5,)),
            pltpu.SemaphoreType.DMA((15,)),
        ],
        compiler_params=pltpu.CompilerParams(
            collective_id=0, has_side_effects=True, vmem_limit_bytes=60 * 1024 * 1024
        ),
    )(coords, probes, u_bases, v_bases)


def solution(mesh):
    return jax.shard_map(
        shards,
        mesh=mesh,
        in_specs=(P(None, "pts"), P(None, "pts"), P(None, "pts"), P(None, "pts")),
        out_specs=(P(None, "pts"), P(None, "pts")),
        check_vma=False,
    )
```

```python
import jax
import jax.numpy as jnp
from jax import lax
from jax.experimental import pallas as pl
from jax.experimental.pallas import tpu as pltpu
from jax.sharding import PartitionSpec as P

MESH = pl.DeviceIdType.MESH
F32 = jnp.float32
BF16 = jnp.bfloat16

LEAF = 256
VMEM_BYTES = 32 * 1024 * 1024
POINTS_HERE = 512
RANKS = 1600
LOW, MID, TOP7, TOP8 = 0, 320, 832, 1088

cell_units = 16.0
length_scale = 4.0
root_three = 1.7320508075688772
nugget = 0.1


def device(x, y, z, c):
    return ((x * 8 + y) * 8 + z) * 2 + c


def nt(a, b):
    return lax.dot_general(a, b, (((1,), (1,)), ((), ())), preferred_element_type=F32)


def nn(a, b):
    return jnp.dot(a, b, preferred_element_type=F32)


def send(src, dst, send_sem, recv_sem, to):
    pltpu.make_async_remote_copy(
        src_ref=src,
        dst_ref=dst,
        send_sem=send_sem,
        recv_sem=recv_sem,
        device_id=(to,),
        device_id_type=MESH,
    ).start()


def wait(ref, sem):
    pltpu.make_async_copy(ref, ref, sem).wait()


def total(ref, n):
    return sum(ref[k].astype(F32) for k in range(n))


def matern(spots, leaf):
    cols = spots[:, leaf * LEAF : (leaf + 1) * LEAF]
    tall = jnp.transpose(cols)
    delta_x = tall[:, 0:1] - cols[0:1, :]
    delta_y = tall[:, 1:2] - cols[1:2, :]
    scaled = (root_three / length_scale) * jnp.sqrt(delta_x * delta_x + delta_y * delta_y)
    row = lax.broadcasted_iota(jnp.int32, (LEAF, LEAF), 0)
    col = lax.broadcasted_iota(jnp.int32, (LEAF, LEAF), 1)
    block = (1.0 + scaled) * jnp.exp(-scaled) + jnp.where(row == col, nugget, 0.0)
    return block.astype(BF16)


def kernel(
    coords_hbm, probes_hbm, u_hbm, v_hbm, out_ref,
    coords, probes, signs, u, v,
    snd_y, snd_z, low_snd, low0,
    ry, rz, py, pz, qy, qz, q1, q2, q3, fin,
    load, s1, s2, s3, sl, rs, cross,
):
    me = lax.axis_index("pts")
    c = me % 2
    z = (me // 2) % 8
    y = (me // 16) % 8
    x = me // 128
    yc = y * 2 + c
    zc = z * 2 + c
    core0 = c == 0
    core1 = c == 1
    z_odd = z % 2 == 1
    owns_8f = jnp.logical_and(core0, y % 2 == 0)
    owns_7 = jnp.logical_and(core0, y % 2 == 1)
    owns_8t = jnp.logical_and(core1, z % 2 == 0)
    owns_45 = jnp.logical_and(core1, z_odd)
    owns_6 = jnp.logical_and(core0, z_odd)
    owns_z = jnp.logical_or(core1, z_odd)
    half = 2 - (x // 2) * 2
    beside = x + 1 - 2 * (x % 2)
    zslot = jnp.where(core1, z, 8 + z // 2)

    loads = [
        (probes_hbm, probes, None),
        (v_hbm, v, (TOP8, 512)),
        (u_hbm, u, (TOP8, 512)),
        (v_hbm, v, (TOP7, 256)),
        (u_hbm, u, (TOP7, 256)),
        (v_hbm, v, (MID, 512)),
        (u_hbm, u, (MID, 512)),
        (v_hbm, v, (LOW, 320)),
        (u_hbm, u, (LOW, 320)),
        (coords_hbm, coords, None),
    ]
    copies = []
    for i, (src, dst, rows) in enumerate(loads):
        if rows is not None:
            src, dst = src.at[pl.ds(*rows)], dst.at[pl.ds(*rows)]
        copies.append(pltpu.make_async_copy(src, dst, load.at[i]))
        copies[-1].start()

    barrier = pltpu.get_barrier_semaphore()

    def greet(to):
        pl.semaphore_signal(barrier, inc=1, device_id=(to,), device_id_type=MESH)

    for j in (4, 3, 5, 2, 6, 1, 7):
        for core in range(2):
            greet(device(x, (y + j) % 8, z, core))
            greet(device(x, y, (z + j) % 8, core))
    for j in (2, 1, 3):
        greet(device((x + j) % 4, y, z, c))
    greet(device(x, y, z, 1 - c))

    copies[0].wait()
    signs[...] = (2 * probes[...] - 1).astype(BF16)

    def keep(part, into, chunks):
        for k, to in enumerate(chunks):
            into[to] = part[:, k * 128 : (k + 1) * 128].astype(BF16)

    copies[1].wait()
    keep(nt(signs[...], v[pl.ds(TOP8, 512), :]), snd_y, (0, 2, 4, 6))
    copies[2].wait()
    keep(nt(signs[...], u[pl.ds(TOP8, 512), :]), snd_z, (0, 2, 4, 6))

    pl.semaphore_wait(barrier, 32)

    def to_y_owners(first, own):
        def one(k, sem):
            at = 2 * k + first
            send(snd_y.at[at], ry.at[yc], s1.at[sem], rs.at[0], device(x, at, z, 0))

        for j in (2, 1, 3):
            one((y // 2 + j) % 4, 0)

        @pl.when(jnp.logical_not(own))
        def _():
            one(y // 2, 1)

        @pl.when(own)
        def _():
            ry[yc] = snd_y[2 * (y // 2) + first]

    def to_z_owners(first, core, own):
        def slot(k):
            return 2 * k + first if core == 1 else 8 + k

        def one(k, sem):
            to = device(x, y, 2 * k + first, core)
            send(snd_z.at[slot(k)], rz.at[zc], s1.at[sem], rs.at[1], to)

        for j in (2, 1, 3):
            one((z // 2 + j) % 4, 0)

        @pl.when(jnp.logical_not(own))
        def _():
            one(z // 2, 1)

        @pl.when(own)
        def _():
            rz[zc] = snd_z[slot(z // 2)]

    to_y_owners(0, owns_8f)
    to_z_owners(0, 1, owns_8t)
    for j in (2, 1, 3):
        pl.semaphore_signal(
            cross, inc=1, device_id=(device((x + j) % 4, y, z, c),), device_id_type=MESH
        )

    copies[3].wait()
    keep(nt(signs[...], v[pl.ds(TOP7, 256), :]), snd_y, (1, 3))
    copies[4].wait()
    keep(nt(signs[...], u[pl.ds(TOP7, 256), :]), snd_y, (5, 7))

    to_y_owners(1, owns_7)

    copies[5].wait()
    keep(nt(signs[...], v[pl.ds(MID, 512), :]), snd_z, (1, 5, 8, 9))
    copies[6].wait()
    keep(nt(signs[...], u[pl.ds(MID, 512), :]), snd_z, (3, 7, 10, 11))

    to_z_owners(1, 1, owns_45)
    to_z_owners(1, 0, owns_6)

    copies[7].wait()
    low_f = nt(signs[...], v[pl.ds(64, 256), :])
    copies[8].wait()
    low_t = nt(signs[...], u[pl.ds(64, 256), :])
    joined = [
        jnp.concatenate([low_f[:, k * 64 : (k + 1) * 64], low_t[:, k * 64 : (k + 1) * 64]], axis=1)
        for k in range(4)
    ]
    low0[...] = joined[0].astype(BF16)
    for k in range(3):
        low_snd[k] = joined[k + 1]
    send(low0, fin.at[20], sl.at[0], rs.at[3], device(x, y, z, 1 - c))
    chip1 = z + 1 - 2 * (z % 2)
    send(low_snd.at[0], q1.at[c], sl.at[1], rs.at[4], device(x, y, chip1, 0))
    send(low_snd.at[0], q1.at[c], sl.at[2], rs.at[4], device(x, y, chip1, 1))
    pair = z // 2
    sib_pair = pair + 1 - 2 * (pair % 2)
    send(low_snd.at[1], q2.at[zc % 4], sl.at[3], rs.at[5], device(x, y, 2 * sib_pair, 0))
    quad = z // 4
    send(low_snd.at[2], q3.at[zc % 8], sl.at[4], rs.at[6], device(x, y, 4 * (1 - quad) + 2, 0))

    @pl.when(core0)
    def _():
        wait(ry.at[pl.ds(0, 15)], rs.at[0])
        py[...] = total(ry, 16).astype(BF16)

    pl.semaphore_wait(cross, 3)

    @pl.when(owns_8f)
    def _():
        for j in (4, 3, 5, 2, 6, 1, 7, 0):
            for h in range(2):
                to = device(half + h, y, (z + j) % 8, 0)
                send(py, qy.at[(x % 2) * 8 + z], s2.at[0], rs.at[2], to)

    @pl.when(owns_7)
    def _():
        for j in (4, 3, 5, 2, 6, 1, 7, 0):
            send(py, qy.at[z], s2.at[0], rs.at[2], device(beside, y, (z + j) % 8, 0))

    @pl.when(owns_z)
    def _():
        wait(rz.at[pl.ds(0, 15)], rs.at[1])
        pz[...] = total(rz, 16).astype(BF16)

    @pl.when(owns_8t)
    def _():
        for j in (4, 3, 5, 2, 6, 1, 7, 0):
            for h in range(2):
                to = device(half + h, (y + j) % 8, z, 1)
                send(pz, qz.at[(x % 2) * 8 + y], s2.at[1], rs.at[7], to)

    def mid_levels(action):
        for n, chosen in (
            (1, jnp.logical_and(owns_45, z < 4)),
            (2, jnp.logical_and(owns_45, z >= 4)),
            (4, owns_6),
        ):
            @pl.when(chosen)
            def _():
                action(n)

    def mid_send(n):
        node = y // n
        first = (node + 1 - 2 * (node % 2)) * n
        for j in range(n):
            send(pz, qz.at[y % n], s2.at[1], rs.at[7], device(x, first + j, z, c))

    mid_levels(mid_send)

    copies[9].wait()
    spots = coords[...].astype(F32) / cell_units
    for leaf in range(2):
        cols = pl.ds(leaf * LEAF, LEAF)
        other = pl.ds((1 - leaf) * LEAF, LEAF)
        near = nn(signs[:, cols], matern(spots, leaf))
        coef_f = nt(signs[:, other], v[pl.ds(0, 64), other]).astype(BF16)
        coef_t = nt(signs[:, other], u[pl.ds(0, 64), other]).astype(BF16)
        out_ref[:16, cols] = near + nn(coef_f, u[pl.ds(0, 64), cols])
        out_ref[16:, cols] = near + nn(coef_t, v[pl.ds(0, 64), cols])

    owner2 = jnp.logical_and(core0, z % 2 == 0)
    owner3 = jnp.logical_and(core0, z % 4 == 2)

    @pl.when(owner2)
    def _():
        wait(q2, rs.at[5])
        fin[22] = total(q2, 4).astype(BF16)
        for j in range(1, 4):
            o = (zc % 4 + j) % 4
            send(fin.at[22], fin.at[22], s3.at[0], rs.at[8], device(x, y, 2 * pair + o // 2, o % 2))

    @pl.when(owner3)
    def _():
        wait(q3, rs.at[6])
        fin[23] = total(q3, 8).astype(BF16)
        for j in range(1, 8):
            o = (zc % 8 + j) % 8
            send(fin.at[23], fin.at[23], s3.at[1], rs.at[9], device(x, y, 4 * quad + o // 2, o % 2))

    def to_z_group(sem):
        for j in (4, 3, 5, 2, 6, 1, 7):
            for core in range(2):
                to = device(x, y, (z + j) % 8, core)
                send(fin.at[8 + zslot], fin.at[8 + zslot], s3.at[2], rs.at[sem], to)
        send(fin.at[8 + zslot], fin.at[8 + zslot], s3.at[2], rs.at[sem], device(x, y, z, 1 - c))

    def to_y_group(sem):
        for j in (4, 3, 5, 2, 6, 1, 7):
            for core in range(2):
                send(fin.at[y], fin.at[y], s3.at[3], rs.at[sem], device(x, (y + j) % 8, z, core))
        send(fin.at[y], fin.at[y], s3.at[3], rs.at[sem], device(x, y, z, 1))

    def mid_sum(n):
        wait(qz.at[pl.ds(0, n)], rs.at[7])
        fin[8 + zslot] = total(qz, n).astype(BF16)
        to_z_group(10)

    mid_levels(mid_sum)

    @pl.when(owns_7)
    def _():
        wait(qy.at[pl.ds(0, 8)], rs.at[2])
        fin[y] = total(qy, 8).astype(BF16)
        to_y_group(11)

    @pl.when(owns_8f)
    def _():
        wait(qy, rs.at[2])
        fin[y] = total(qy, 16).astype(BF16)
        to_y_group(12)

    @pl.when(owns_8t)
    def _():
        wait(qz, rs.at[7])
        fin[8 + zslot] = total(qz, 16).astype(BF16)
        to_z_group(13)

    wait(low0, rs.at[3])
    wait(q1, rs.at[4])
    fin[21] = total(q1, 2).astype(BF16)

    @pl.when(jnp.logical_not(owner2))
    def _():
        wait(low0, rs.at[8])

    @pl.when(jnp.logical_not(owner3))
    def _():
        wait(low0, rs.at[9])

    low = [fin[20 + k] for k in range(4)]
    low_f = jnp.concatenate([part[:, :64] for part in low], axis=1)
    low_t = jnp.concatenate([part[:, 64:] for part in low], axis=1)
    out_ref[:16, :] += nn(low_f, u[pl.ds(64, 256), :])
    out_ref[16:, :] += nn(low_t, v[pl.ds(64, 256), :])

    def await_chunks(n, sem, own):
        @pl.when(own)
        def _():
            wait(fin.at[pl.ds(0, n - 1)], rs.at[sem])

        @pl.when(jnp.logical_not(own))
        def _():
            wait(fin.at[pl.ds(0, n)], rs.at[sem])

    await_chunks(8, 10, z_odd)

    def joint(chunks):
        return jnp.concatenate([fin[k] for k in chunks], axis=1)

    out_ref[:16, :] += nn(joint((9, 13, 16, 17)), u[pl.ds(MID, 512), :])
    out_ref[16:, :] += nn(joint((11, 15, 18, 19)), v[pl.ds(MID, 512), :])

    await_chunks(4, 11, owns_7)

    out_ref[:16, :] += nn(joint((1, 3)), u[pl.ds(TOP7, 256), :])
    out_ref[16:, :] += nn(joint((5, 7)), v[pl.ds(TOP7, 256), :])

    await_chunks(4, 12, owns_8f)
    await_chunks(4, 13, owns_8t)

    out_ref[:16, :] += nn(joint((0, 2, 4, 6)), u[pl.ds(TOP8, 512), :])
    out_ref[16:, :] += nn(joint((8, 10, 12, 14)), v[pl.ds(TOP8, 512), :])

    wait(ry.at[pl.ds(0, 15)], s1.at[0])

    @pl.when(owns_6)
    def _():
        wait(ry.at[pl.ds(0, 3)], s1.at[1])

    @pl.when(jnp.logical_not(owns_6))
    def _():
        wait(ry.at[pl.ds(0, 4)], s1.at[1])

    wait(low0, sl.at[0])
    for k in range(1, 5):
        wait(low_snd.at[0], sl.at[k])

    @pl.when(owns_8f)
    def _():
        wait(qy, s2.at[0])

    @pl.when(owns_7)
    def _():
        wait(qy.at[pl.ds(0, 8)], s2.at[0])

    @pl.when(owns_8t)
    def _():
        wait(qz, s2.at[1])

    mid_levels(lambda n: wait(qz.at[pl.ds(0, n)], s2.at[1]))

    @pl.when(core0)
    def _():
        wait(fin.at[pl.ds(0, 15)], s3.at[3])

    @pl.when(owns_z)
    def _():
        wait(fin.at[pl.ds(0, 15)], s3.at[2])

    @pl.when(owner2)
    def _():
        wait(fin.at[pl.ds(0, 3)], s3.at[0])

    @pl.when(owner3)
    def _():
        wait(fin.at[pl.ds(0, 7)], s3.at[1])


def shards(coords, probes, u_bases, v_bases):
    tile = (16, 128)
    operands = [
        pltpu.with_memory_space_constraint(a, pltpu.HBM) for a in (coords, probes, u_bases, v_bases)
    ]
    both = pl.pallas_call(
        kernel,
        out_shape=jax.ShapeDtypeStruct((32, POINTS_HERE), F32),
        in_specs=[pl.BlockSpec(memory_space=pl.ANY)] * 4,
        out_specs=pl.BlockSpec(memory_space=pltpu.VMEM),
        scratch_shapes=[
            pltpu.VMEM((2, POINTS_HERE), jnp.int32),
            pltpu.VMEM((16, POINTS_HERE), jnp.int32),
            pltpu.VMEM((16, POINTS_HERE), BF16),
            pltpu.VMEM((RANKS, POINTS_HERE), BF16),
            pltpu.VMEM((RANKS, POINTS_HERE), BF16),
            pltpu.VMEM((8,) + tile, BF16),
            pltpu.VMEM((12,) + tile, BF16),
            pltpu.VMEM((3,) + tile, F32),
            pltpu.VMEM(tile, BF16),
            pltpu.VMEM((16,) + tile, BF16),
            pltpu.VMEM((16,) + tile, BF16),
            pltpu.VMEM(tile, BF16),
            pltpu.VMEM(tile, BF16),
            pltpu.VMEM((16,) + tile, BF16),
            pltpu.VMEM((16,) + tile, BF16),
            pltpu.VMEM((2,) + tile, F32),
            pltpu.VMEM((4,) + tile, F32),
            pltpu.VMEM((8,) + tile, F32),
            pltpu.VMEM((24,) + tile, BF16),
            pltpu.SemaphoreType.DMA((10,)),
            pltpu.SemaphoreType.DMA((2,)),
            pltpu.SemaphoreType.DMA((2,)),
            pltpu.SemaphoreType.DMA((4,)),
            pltpu.SemaphoreType.DMA((5,)),
            pltpu.SemaphoreType.DMA((14,)),
            pltpu.SemaphoreType.REGULAR,
        ],
        compiler_params=pltpu.CompilerParams(
            collective_id=0, has_side_effects=True, vmem_limit_bytes=VMEM_BYTES
        ),
    )(*operands)
    return both[:16], both[16:]


def solution(mesh):
    return jax.shard_map(
        shards,
        mesh=mesh,
        in_specs=(P(None, "pts"), P(None, "pts"), P(None, "pts"), P(None, "pts")),
        out_specs=(P(None, "pts"), P(None, "pts")),
        check_vma=False,
    )
```

```python
import jax
import jax.numpy as jnp
from jax import lax
from jax.experimental import pallas as pl
from jax.experimental.pallas import tpu as pltpu
from jax.sharding import PartitionSpec as P

MESH = pl.DeviceIdType.MESH
F32 = jnp.float32
BF16 = jnp.bfloat16

LEAF = 256
VMEM_BYTES = 32 * 1024 * 1024
POINTS_HERE = 512
RANKS = 1600
LOW, MID, TOP7, TOP8 = 0, 320, 832, 1088

cell_units = 16.0
length_scale = 4.0
root_three = 1.7320508075688772
nugget = 0.1


def device(x, y, z, c):
    return ((x * 8 + y) * 8 + z) * 2 + c


def nt(a, b):
    return lax.dot_general(a, b, (((1,), (1,)), ((), ())), preferred_element_type=F32)


def nn(a, b):
    return jnp.dot(a, b, preferred_element_type=F32)


def send(src, dst, send_sem, recv_sem, to):
    pltpu.make_async_remote_copy(
        src_ref=src,
        dst_ref=dst,
        send_sem=send_sem,
        recv_sem=recv_sem,
        device_id=(to,),
        device_id_type=MESH,
    ).start()


def wait(ref, sem):
    pltpu.make_async_copy(ref, ref, sem).wait()


def matern(spots, leaf):
    cols = spots[:, leaf * LEAF : (leaf + 1) * LEAF]
    tall = jnp.transpose(cols)
    delta_x = tall[:, 0:1] - cols[0:1, :]
    delta_y = tall[:, 1:2] - cols[1:2, :]
    scaled = (root_three / length_scale) * jnp.sqrt(delta_x * delta_x + delta_y * delta_y)
    row = lax.broadcasted_iota(jnp.int32, (LEAF, LEAF), 0)
    col = lax.broadcasted_iota(jnp.int32, (LEAF, LEAF), 1)
    block = (1.0 + scaled) * jnp.exp(-scaled) + jnp.where(row == col, nugget, 0.0)
    return block.astype(BF16)


def kernel(
    coords_hbm, probes_hbm, u_hbm, v_hbm, out_ref,
    coords, probes, signs, u, v,
    snd, low0, got, mine, q8, q7, qm, low_out, fin, fin0,
    load, s1, s2, s3, sl, rs,
):
    me = lax.axis_index("pts")
    c = me % 2
    z = (me // 2) % 8
    y = (me // 16) % 8
    x = me // 128
    zc = z * 2 + c
    owns = zc < 8
    owns_8 = zc < 4
    owns_47 = jnp.logical_and(zc >= 4, zc < 8)
    half = 2 - (x // 2) * 2
    beside = x + 1 - 2 * (x % 2)

    def member(place):
        return device(x, y, place // 2, place % 2)

    loads = [
        (probes_hbm, probes, None),
        (v_hbm, v, (TOP8, 512)),
        (u_hbm, u, (TOP8, 512)),
        (v_hbm, v, (MID, 512)),
        (u_hbm, u, (MID, 512)),
        (v_hbm, v, (TOP7, 256)),
        (u_hbm, u, (TOP7, 256)),
        (v_hbm, v, (LOW, 320)),
        (u_hbm, u, (LOW, 320)),
        (coords_hbm, coords, None),
    ]
    copies = []
    for i, (src, dst, rows) in enumerate(loads):
        if rows is not None:
            src, dst = src.at[pl.ds(*rows)], dst.at[pl.ds(*rows)]
        copies.append(pltpu.make_async_copy(src, dst, load.at[i]))
        copies[-1].start()

    barrier = pltpu.get_barrier_semaphore()

    def greet(to):
        pl.semaphore_signal(barrier, inc=1, device_id=(to,), device_id_type=MESH)

    @pl.when(owns)
    def _():
        for j in range(1, 16):
            greet(member((zc + j) % 16))

    @pl.when(jnp.logical_not(owns))
    def _():
        greet(device(x, y, z, 1 - c))

    @pl.when(owns_8)
    def _():
        for h in range(2):
            for j in range(8):
                greet(device(half + h, j, z, c))

    @pl.when(owns_47)
    def _():
        for j in range(8):
            greet(device(beside, j, z, c))
        for j in range(1, 8):
            greet(device(x, (y + j) % 8, z, c))

    copies[0].wait()
    signs[...] = (2 * probes[...] - 1).astype(BF16)

    def keep(part, places):
        for k, (owner, row) in enumerate(places):
            snd[owner, row] = part[:, k * 128 : (k + 1) * 128].astype(BF16)

    def to_owners(first, rows):
        def one(place, sem):
            send(snd.at[place, rows], got.at[zc, rows], s1.at[sem], rs.at[0], member(place))

        for j in range(1, 4):
            one(first + (zc + j) % 4, 0)

        own = jnp.logical_and(zc >= first, zc < first + 4)

        @pl.when(jnp.logical_not(own))
        def _():
            one(first + zc % 4, 1)

        @pl.when(own)
        def _():
            got[zc, rows] = snd[zc, rows]

    copies[1].wait()
    keep(nt(signs[...], v[pl.ds(TOP8, 512), :]), [(k, 0) for k in range(4)])

    @pl.when(owns_8)
    def _():
        pl.semaphore_wait(barrier, 23)

    @pl.when(owns_47)
    def _():
        pl.semaphore_wait(barrier, 22)

    @pl.when(jnp.logical_not(owns))
    def _():
        pl.semaphore_wait(barrier, 9)

    to_owners(0, pl.ds(0, 1))

    copies[2].wait()
    keep(nt(signs[...], u[pl.ds(TOP8, 512), :]), [(k, 1) for k in range(4)])

    to_owners(0, pl.ds(1, 1))

    copies[3].wait()
    keep(nt(signs[...], v[pl.ds(MID, 512), :]), [(4, 1), (5, 1), (6, 1), (6, 2)])
    copies[4].wait()
    keep(nt(signs[...], u[pl.ds(MID, 512), :]), [(4, 2), (5, 2), (7, 1), (7, 2)])

    copies[5].wait()
    keep(nt(signs[...], v[pl.ds(TOP7, 256), :]), [(4, 0), (5, 0)])
    copies[6].wait()
    keep(nt(signs[...], u[pl.ds(TOP7, 256), :]), [(6, 0), (7, 0)])

    to_owners(4, pl.ds(0, 3))

    copies[7].wait()
    low_f = nt(signs[...], v[pl.ds(64, 256), :])
    copies[8].wait()
    low_t = nt(signs[...], u[pl.ds(64, 256), :])
    joined = [
        jnp.concatenate(
            [low_f[:, k * 64 : (k + 1) * 64], low_t[:, k * 64 : (k + 1) * 64]], axis=1
        ).astype(BF16)
        for k in range(4)
    ]
    low0[...] = joined[0]
    send(low0, fin0, sl, rs.at[2], device(x, y, z, 1 - c))
    for owner in range(3):
        snd[owner, 2] = joined[3 - owner]

        @pl.when(zc == owner)
        def _():
            got[zc, 2] = snd[owner, 2]

        @pl.when(zc != owner)
        def _():
            send(snd.at[owner, 2], got.at[zc, 2], s1.at[2], rs.at[1], member(owner))

    copies[9].wait()
    spots = coords[...].astype(F32) / cell_units
    for leaf in range(2):
        cols = pl.ds(leaf * LEAF, LEAF)
        other = pl.ds((1 - leaf) * LEAF, LEAF)
        near = nn(signs[:, cols], matern(spots, leaf))
        coef_f = nt(signs[:, other], v[pl.ds(0, 64), other]).astype(BF16)
        coef_t = nt(signs[:, other], u[pl.ds(0, 64), other]).astype(BF16)
        out_ref[:16, cols] = near + nn(coef_f, u[pl.ds(0, 64), cols])
        out_ref[16:, cols] = near + nn(coef_t, v[pl.ds(0, 64), cols])

    def total(parts):
        return sum(part.astype(F32) for part in parts).astype(BF16)

    @pl.when(owns_8)
    def _():
        wait(got.at[pl.ds(0, 10)], rs.at[0])
        for a in range(2):
            mine[a] = total(got[k, a] for k in range(16))

    @pl.when(owns_47)
    def _():
        wait(got.at[pl.ds(0, 15)], rs.at[0])
        for a in range(3):
            mine[a] = total(got[k, a] for k in range(16))

    @pl.when(owns_8)
    def _():
        for j in (0, 1, 7, 2, 6, 3, 5, 4):
            for h in range(2):
                to = device(half + h, j, z, c)
                send(mine.at[pl.ds(0, 2)], q8.at[(x % 2) * 8 + y], s2.at[0], rs.at[3], to)

    @pl.when(owns_47)
    def _():
        for j in (0, 1, 7, 2, 6, 3, 5, 4):
            send(mine.at[0], q7.at[y], s2.at[1], rs.at[4], device(beside, j, z, c))

    def mid_levels(action):
        for n, chosen in ((1, zc == 4), (2, zc == 5), (4, jnp.logical_and(zc >= 6, zc < 8))):
            @pl.when(chosen)
            def _():
                action(n)

    def mid_send(n):
        node = y // n
        first = (node + 1 - 2 * (node % 2)) * n
        for j in range(n):
            send(
                mine.at[pl.ds(1, 2)], qm.at[y % n], s2.at[2], rs.at[5], device(x, first + j, z, c)
            )

    mid_levels(mid_send)

    for owner, size in ((0, 8), (1, 4), (2, 2)):
        @pl.when(zc == owner)
        def _():
            wait(got.at[pl.ds(0, 5)], rs.at[1])
            groups = 16 // size
            for g in range(groups):
                sib = g ^ 1
                low_out[g] = total(got[k, 2] for k in range(sib * size, (sib + 1) * size))
            fin[owner, 2] = low_out[owner // size]
            for place in range(16):
                if place != owner:
                    send(
                        low_out.at[place // size], fin.at[owner, 2], s3.at[0], rs.at[6 + owner],
                        member(place),
                    )

    def hand_out(rows, send_sem, recv_sem, first):
        def one(place):
            send(fin.at[zc, rows], fin.at[zc, rows], s3.at[send_sem], rs.at[recv_sem], member(place))

        for place in range(first):
            one(place)
        for j in range(1, 4):
            one(first + (zc + j) % 4)
        for place in range(first + 4, 16):
            one(place)

    def mid_sum(n):
        wait(qm.at[pl.ds(0, n)], rs.at[5])
        for a in range(2):
            fin[zc, 1 + a] = total(qm[k, a] for k in range(n))
        hand_out(pl.ds(1, 2), 1, 9, 4)

    mid_levels(mid_sum)

    @pl.when(owns_47)
    def _():
        wait(q7, rs.at[4])
        fin[zc, 0] = total(q7[k] for k in range(8))
        hand_out(pl.ds(0, 1), 2, 10, 4)

    @pl.when(owns_8)
    def _():
        wait(q8, rs.at[3])
        for a in range(2):
            fin[zc, a] = total(q8[k, a] for k in range(16))
        hand_out(pl.ds(0, 2), 3, 11, 0)

    wait(low0, rs.at[2])
    for owner in range(3):
        @pl.when(zc != owner)
        def _():
            wait(low0, rs.at[6 + owner])

    low = [fin0[...]] + [fin[owner, 2] for owner in (2, 1, 0)]
    low_f = jnp.concatenate([part[:, :64] for part in low], axis=1)
    low_t = jnp.concatenate([part[:, 64:] for part in low], axis=1)
    out_ref[:16, :] += nn(low_f, u[pl.ds(64, 256), :])
    out_ref[16:, :] += nn(low_t, v[pl.ds(64, 256), :])

    def await_chunks(ref, n, sem, own):
        @pl.when(own)
        def _():
            wait(ref.at[pl.ds(0, n - n // 4)], rs.at[sem])

        @pl.when(jnp.logical_not(own))
        def _():
            wait(ref.at[pl.ds(0, n)], rs.at[sem])

    await_chunks(qm, 4, 9, owns_47)

    def joint(places):
        return jnp.concatenate([fin[owner, row] for owner, row in places], axis=1)

    out_ref[:16, :] += nn(joint([(4, 1), (5, 1), (6, 1), (6, 2)]), u[pl.ds(MID, 512), :])
    out_ref[16:, :] += nn(joint([(4, 2), (5, 2), (7, 1), (7, 2)]), v[pl.ds(MID, 512), :])

    await_chunks(q7, 4, 10, owns_47)

    out_ref[:16, :] += nn(joint([(4, 0), (5, 0)]), u[pl.ds(TOP7, 256), :])
    out_ref[16:, :] += nn(joint([(6, 0), (7, 0)]), v[pl.ds(TOP7, 256), :])

    await_chunks(q8, 4, 11, owns_8)

    out_ref[:16, :] += nn(joint([(k, 0) for k in range(4)]), u[pl.ds(TOP8, 512), :])
    out_ref[16:, :] += nn(joint([(k, 1) for k in range(4)]), v[pl.ds(TOP8, 512), :])

    wait(got.at[pl.ds(0, 5)], s1.at[0])
    wait(low0, sl)

    @pl.when(jnp.logical_not(owns))
    def _():
        wait(got.at[0], s1.at[1])
        wait(q7.at[pl.ds(0, 2)], s1.at[1])

    @pl.when(owns_8)
    def _():
        wait(got.at[0], s1.at[1])
        wait(q8, s2.at[0])
        wait(got.at[pl.ds(0, 10)], s3.at[3])

    @pl.when(owns_47)
    def _():
        wait(q7.at[pl.ds(0, 2)], s1.at[1])
        wait(q7, s2.at[1])
        wait(got.at[pl.ds(0, 10)], s3.at[1])
        wait(got.at[pl.ds(0, 5)], s3.at[2])

    mid_levels(lambda n: wait(qm.at[pl.ds(0, n)], s2.at[2]))

    @pl.when(zc < 3)
    def _():
        wait(q7.at[pl.ds(0, 2)], s1.at[2])
        wait(got.at[pl.ds(0, 5)], s3.at[0])

    @pl.when(zc >= 3)
    def _():
        wait(q7.at[pl.ds(0, 3)], s1.at[2])


def shards(coords, probes, u_bases, v_bases):
    tile = (16, 128)
    operands = [
        pltpu.with_memory_space_constraint(a, pltpu.HBM) for a in (coords, probes, u_bases, v_bases)
    ]
    both = pl.pallas_call(
        kernel,
        out_shape=jax.ShapeDtypeStruct((32, POINTS_HERE), F32),
        in_specs=[pl.BlockSpec(memory_space=pl.ANY)] * 4,
        out_specs=pl.BlockSpec(memory_space=pltpu.VMEM),
        scratch_shapes=[
            pltpu.VMEM((2, POINTS_HERE), jnp.int32),
            pltpu.VMEM((16, POINTS_HERE), jnp.int32),
            pltpu.VMEM((16, POINTS_HERE), BF16),
            pltpu.VMEM((RANKS, POINTS_HERE), BF16),
            pltpu.VMEM((RANKS, POINTS_HERE), BF16),
            pltpu.VMEM((8, 3) + tile, BF16),
            pltpu.VMEM(tile, BF16),
            pltpu.VMEM((16, 3) + tile, BF16),
            pltpu.VMEM((3,) + tile, BF16),
            pltpu.VMEM((16, 2) + tile, BF16),
            pltpu.VMEM((8,) + tile, BF16),
            pltpu.VMEM((4, 2) + tile, BF16),
            pltpu.VMEM((8,) + tile, BF16),
            pltpu.VMEM((8, 3) + tile, BF16),
            pltpu.VMEM(tile, BF16),
            pltpu.SemaphoreType.DMA((10,)),
            pltpu.SemaphoreType.DMA((3,)),
            pltpu.SemaphoreType.DMA((3,)),
            pltpu.SemaphoreType.DMA((4,)),
            pltpu.SemaphoreType.DMA,
            pltpu.SemaphoreType.DMA((12,)),
        ],
        compiler_params=pltpu.CompilerParams(
            collective_id=0, has_side_effects=True, vmem_limit_bytes=VMEM_BYTES
        ),
    )(*operands)
    return both[:16], both[16:]


def solution(mesh):
    return jax.shard_map(
        shards,
        mesh=mesh,
        in_specs=(P(None, "pts"), P(None, "pts"), P(None, "pts"), P(None, "pts")),
        out_specs=(P(None, "pts"), P(None, "pts")),
        check_vma=False,
    )
```

```python
import jax
import jax.numpy as jnp
from jax import lax
from jax.experimental import pallas as pl
from jax.experimental.pallas import tpu as pltpu
from jax.sharding import PartitionSpec as P

MESH = pl.DeviceIdType.MESH
F32 = jnp.float32
BF16 = jnp.bfloat16

LEAF = 256
VMEM_BYTES = 32 * 1024 * 1024
POINTS_HERE = 512
RANKS = 1600
LOW, MID, TOP67, TOP8 = 0, 320, 576, 1088

cell_units = 16.0
length_scale = 4.0
root_three = 1.7320508075688772
nugget = 0.1


def device(x, y, z, c):
    return ((x * 8 + y) * 8 + z) * 2 + c


def nt(a, b):
    return lax.dot_general(a, b, (((1,), (1,)), ((), ())), preferred_element_type=F32)


def nn(a, b):
    return jnp.dot(a, b, preferred_element_type=F32)


def send(src, dst, send_sem, recv_sem, to):
    pltpu.make_async_remote_copy(
        src_ref=src,
        dst_ref=dst,
        send_sem=send_sem,
        recv_sem=recv_sem,
        device_id=(to,),
        device_id_type=MESH,
    ).start()


def wait(ref, sem):
    pltpu.make_async_copy(ref, ref, sem).wait()


def matern(spots, leaf):
    cols = spots[:, leaf * LEAF : (leaf + 1) * LEAF]
    tall = jnp.transpose(cols)
    delta_x = tall[:, 0:1] - cols[0:1, :]
    delta_y = tall[:, 1:2] - cols[1:2, :]
    scaled = (root_three / length_scale) * jnp.sqrt(delta_x * delta_x + delta_y * delta_y)
    row = lax.broadcasted_iota(jnp.int32, (LEAF, LEAF), 0)
    col = lax.broadcasted_iota(jnp.int32, (LEAF, LEAF), 1)
    block = (1.0 + scaled) * jnp.exp(-scaled) + jnp.where(row == col, nugget, 0.0)
    return block.astype(BF16)


def kernel(
    coords_hbm, probes_hbm, u_hbm, v_hbm, out_ref,
    coords, probes, signs, w,
    give, take, snd, low0, got, mine, q8, q7, q6, q45, low_out, fin, fin0,
    load, sent, rx, rs,
):
    me = lax.axis_index("pts")
    c = me % 2
    z = (me // 2) % 8
    y = (me // 16) % 8
    x = me // 128
    core0 = c == 0
    owns = z < 4
    owns_8 = z < 2
    owns_67 = jnp.logical_and(z >= 2, z < 4)
    half = 2 - (x // 2) * 2
    beside = x + 1 - 2 * (x % 2)
    partner = device(x, y, z, 1 - c)
    v, u = w.at[0], w.at[1]
    other, own = w.at[1 - c], w.at[c]

    def chunks(n):
        return q8.at[pl.ds(0, n // 2)] if n % 2 == 0 else q8.at[pl.ds(0, n), 0]

    pieces = [(TOP8, 512), (TOP67, 512), (LOW, 576)]

    def load_bases(sources):
        for i, rows in enumerate(pieces):
            for (src, dst), sem in zip(sources, ((0, 1), (1, 2), (3, 3))[i]):
                pltpu.make_async_copy(
                    src.at[pl.ds(*rows)], dst.at[pl.ds(*rows)], load.at[sem]
                ).start()

    probes_in = pltpu.make_async_copy(probes_hbm, probes, load.at[0])
    probes_in.start()
    coords_in = pltpu.make_async_copy(coords_hbm, coords, load.at[3])

    @pl.when(core0)
    def _():
        load_bases([(u_hbm, u), (v_hbm, v)])

    @pl.when(c == 1)
    def _():
        load_bases([(v_hbm, v), (u_hbm, u)])

    coords_in.start()

    def await_rows(piece, sem):
        wait(v.at[pl.ds(*pieces[piece])], load.at[sem])

    barrier = pltpu.get_barrier_semaphore()

    def greet(to):
        pl.semaphore_signal(barrier, inc=1, device_id=(to,), device_id_type=MESH)

    greet(partner)

    @pl.when(owns)
    def _():
        for j in range(1, 8):
            greet(device(x, y, (z + j) % 8, c))

    @pl.when(owns_8)
    def _():
        for h in range(2):
            for j in range(8):
                greet(device(half + h, j, z, c))

    def siblings(n):
        node = y // n
        first = (node + 1 - 2 * (node % 2)) * n
        return [device(x, first + j, z, c) for j in range(n)]

    @pl.when(z == 1)
    def _():
        for to in siblings(1) + siblings(2):
            greet(to)

    @pl.when(z == 2)
    def _():
        for j in range(8):
            greet(device(beside, j, z, c))

    @pl.when(z == 3)
    def _():
        for to in siblings(4):
            greet(to)

    probes_in.wait()
    await_rows(0, 0)
    signs[...] = (2 * probes[...] - 1).astype(BF16)

    def coefs(bases, first, count):
        return nt(signs[...], bases[pl.ds(first, count), :])

    def lanes(part, k):
        return part[:, k * 128 : (k + 1) * 128]

    def hand_over(first, part, count, i):
        for k in range(count):
            give[first + k] = lanes(part, k)
        rows = pl.ds(first, count)
        send(give.at[rows], take.at[rows], sent, rx.at[i], partner)

    other_8 = coefs(other, TOP8, 512)

    for place, count in enumerate((20, 23, 12, 8)):
        @pl.when(z == place)
        def _():
            pl.semaphore_wait(barrier, count)

    @pl.when(jnp.logical_not(owns))
    def _():
        pl.semaphore_wait(barrier, 5)

    hand_over(0, other_8, 4, 0)
    await_rows(0, 1)
    await_rows(1, 1)
    hand_over(4, coefs(other, TOP67, 512), 4, 1)

    def to_owner(place, rows, recv_sem):
        @pl.when(z != place)
        def _():
            send(
                snd.at[place, rows], got.at[z, rows], sent, rs.at[recv_sem],
                device(x, y, place, c),
            )

        @pl.when(z == place)
        def _():
            got[place, rows] = snd[place, rows]

    own_8 = coefs(own, TOP8, 512)

    wait(take.at[pl.ds(0, 4)], rx.at[0])
    for k in range(4):
        snd[k // 2, k % 2] = (lanes(own_8, k) + take[k]).astype(BF16)
    for place in range(2):
        to_owner(place, pl.ds(0, 2), 0)

    await_rows(1, 2)
    own_67 = coefs(own, TOP67, 512)

    wait(take.at[pl.ds(4, 4)], rx.at[1])
    for k in range(4):
        snd[3 - k // 2, k % 2] = (lanes(own_67, k) + take[4 + k]).astype(BF16)
    for place in (2, 3):
        to_owner(place, pl.ds(0, 2), 0)

    coords_in.wait()
    await_rows(2, 3)
    await_rows(2, 3)
    spots = coords[...].astype(F32) / cell_units
    for leaf in range(2):
        cols = pl.ds(leaf * LEAF, LEAF)
        across = pl.ds((1 - leaf) * LEAF, LEAF)
        near = nn(signs[:, cols], matern(spots, leaf))
        coef_f = nt(signs[:, across], v[pl.ds(0, 64), across]).astype(BF16)
        coef_t = nt(signs[:, across], u[pl.ds(0, 64), across]).astype(BF16)
        out_ref[:16, cols] = near + nn(coef_f, u[pl.ds(0, 64), cols])
        out_ref[16:, cols] = near + nn(coef_t, v[pl.ds(0, 64), cols])

    other_low = coefs(other, 64, 512)
    hand_over(8, other_low, 4, 2)
    own_low = coefs(own, 64, 512)
    f_0 = jnp.where(core0, own_low[:, :64], other_low[:, :64])
    t_0 = jnp.where(core0, other_low[:, :64], own_low[:, :64])
    low0[...] = jnp.concatenate([f_0, t_0], axis=1).astype(BF16)
    send(low0, fin0, sent, rs.at[2], partner)
    wait(take.at[pl.ds(8, 4)], rx.at[2])
    for k, (place, row) in enumerate(((0, 2), (1, 2), (1, 3), (1, 4))):
        snd[place, row] = (lanes(own_low, k) + take[8 + k]).astype(BF16)
    to_owner(1, pl.ds(2, 3), 1)
    to_owner(0, pl.ds(2, 1), 1)

    def total(parts):
        return sum(part.astype(F32) for part in parts)

    @pl.when(owns)
    def _():
        wait(q8.at[pl.ds(0, 7)], rs.at[0])
        for a in range(2):
            mine[a] = total(got[k, a] for k in range(8)).astype(BF16)

    @pl.when(owns_8)
    def _():
        for j in (0, 1, 7, 2, 6, 3, 5, 4):
            for h in range(2):
                to = device(half + h, j, z, c)
                send(mine.at[pl.ds(0, 2)], q8.at[(x % 2) * 8 + y], sent, rs.at[3], to)

    @pl.when(z == 2)
    def _():
        for j in (0, 1, 7, 2, 6, 3, 5, 4):
            send(mine.at[pl.ds(0, 2)], q7.at[y], sent, rs.at[3], device(beside, j, z, c))

    @pl.when(z == 3)
    def _():
        for to in siblings(4):
            send(mine.at[pl.ds(0, 2)], q6.at[y % 4], sent, rs.at[3], to)

    def hand_out_low(own_place, source, recv_sem):
        for place in (0, 1, 2, 3, 4, 5, 6, 7):
            if place == own_place:
                fin[c, own_place, 2] = source(place)[...]
                send(source(place), fin.at[c, own_place, 2], sent, rs.at[recv_sem], partner)
            else:
                for core in range(2):
                    to = device(x, y, place, core)
                    send(source(place), fin.at[c, own_place, 2], sent, rs.at[recv_sem], to)

    @pl.when(z == 0)
    def _():
        wait(chunks(7), rs.at[1])
        hand_out_low(0, lambda place: got.at[place ^ 1, 2], 2)

    @pl.when(z == 1)
    def _():
        wait(got.at[pl.ds(0, 7), pl.ds(0, 3)], rs.at[1])
        for a in (3, 4):
            mine[a] = total(got[k, a] for k in range(8)).astype(BF16)
        for to in siblings(1):
            send(mine.at[3], q45.at[0], sent, rs.at[4], to)
        for to in siblings(2):
            send(mine.at[4], q45.at[1 + y % 2], sent, rs.at[4], to)
        pairs = [total(got[2 * k + i, 2] for i in range(2)) for k in range(4)]
        quads = [pairs[0] + pairs[1], pairs[2] + pairs[3]]
        lane = lax.broadcasted_iota(jnp.int32, (16, 128), 1)
        for k in range(4):
            low_out[k] = jnp.where(lane < 64, pairs[k ^ 1], quads[1 - k // 2]).astype(BF16)
        hand_out_low(1, lambda place: low_out.at[place // 2], 2)

    def hand_out(own_place, rows, recv_sem, places):
        src = fin.at[c, own_place, rows]
        for place in places:
            if place == own_place:
                send(src, src, sent, rs.at[recv_sem], partner)
            else:
                for core in range(2):
                    to = device(x, y, place, core)
                    send(src, src, sent, rs.at[recv_sem], to)

    @pl.when(z == 1)
    def _():
        wait(q45, rs.at[4])
        fin[c, 1, 3] = q45[0]
        fin[c, 1, 4] = total(q45[1 + k] for k in range(2)).astype(BF16)
        hand_out(1, pl.ds(3, 2), 5, (0, 1, 2, 3, 7, 4, 6, 5))

    @pl.when(z == 2)
    def _():
        wait(q7, rs.at[3])
        for a in range(2):
            fin[c, 2, a] = total(q7[k, a] for k in range(8)).astype(BF16)
        hand_out(2, pl.ds(0, 2), 6, (0, 1, 2, 3, 7, 4, 6, 5))

    @pl.when(z == 3)
    def _():
        wait(q6, rs.at[3])
        for a in range(2):
            fin[c, 3, a] = total(q6[k, a] for k in range(4)).astype(BF16)
        hand_out(3, pl.ds(0, 2), 6, (0, 1, 2, 3, 7, 4, 6, 5))

    for own_place in range(2):
        @pl.when(z == own_place)
        def _():
            wait(q8, rs.at[3])
            for a in range(2):
                fin[c, own_place, a] = total(q8[k, a] for k in range(16)).astype(BF16)
            hand_out(own_place, pl.ds(0, 2), 7, (0, 1, 2, 3, 7, 4, 6, 5))

    def await_chunks(most, least, sem, is_own):
        @pl.when(is_own)
        def _():
            wait(chunks(least), rs.at[sem])

        @pl.when(jnp.logical_not(is_own))
        def _():
            wait(chunks(most), rs.at[sem])

    await_chunks(5, 4, 2, owns_8)
    low_f = jnp.concatenate([fin0[:, :64], fin[0, 0, 2][:, 64:], fin[0, 1, 2]], axis=1)
    low_t = jnp.concatenate([fin0[:, 64:], fin[1, 0, 2][:, 64:], fin[1, 1, 2]], axis=1)
    out_ref[:16, :] += nn(low_f, u[pl.ds(64, 256), :])
    out_ref[16:, :] += nn(low_t, v[pl.ds(64, 256), :])

    await_chunks(4, 2, 5, z == 1)

    def add(places, first):
        count = 128 * len(places)
        for kind, bases in ((0, u), (1, v)):
            coefs_here = jnp.concatenate([fin[kind, place, row] for place, row in places], axis=1)
            out_ref[kind * 16 : kind * 16 + 16, :] += nn(coefs_here, bases[pl.ds(first, count), :])

    add([(1, 3), (1, 4)], MID)

    await_chunks(8, 6, 6, owns_67)

    add([(3, 0), (3, 1), (2, 0), (2, 1)], TOP67)

    await_chunks(8, 6, 7, owns_8)

    add([(0, 0), (0, 1), (1, 0), (1, 1)], TOP8)

    wait(give, sent)

    def left(*sizes):
        for n in sizes:
            wait(chunks(n), sent)

    @pl.when(jnp.logical_not(owns))
    def _():
        left(13)

    @pl.when(z == 0)
    def _():
        left(10, 32, 15, 30)

    @pl.when(z == 1)
    def _():
        left(8, 32, 3, 15, 30, 30)

    @pl.when(z == 2)
    def _():
        left(11, 16, 30)

    @pl.when(z == 3)
    def _():
        left(11, 8, 30)


def shards(coords, probes, u_bases, v_bases):
    tile = (16, 128)
    operands = [
        pltpu.with_memory_space_constraint(a, pltpu.HBM) for a in (coords, probes, u_bases, v_bases)
    ]
    both = pl.pallas_call(
        kernel,
        out_shape=jax.ShapeDtypeStruct((32, POINTS_HERE), F32),
        in_specs=[pl.BlockSpec(memory_space=pl.ANY)] * 4,
        out_specs=pl.BlockSpec(memory_space=pltpu.VMEM),
        scratch_shapes=[
            pltpu.VMEM((2, POINTS_HERE), jnp.int32),
            pltpu.VMEM((16, POINTS_HERE), jnp.int32),
            pltpu.VMEM((16, POINTS_HERE), BF16),
            pltpu.VMEM((2, RANKS, POINTS_HERE), BF16),
            pltpu.VMEM((12,) + tile, F32),
            pltpu.VMEM((12,) + tile, F32),
            pltpu.VMEM((4, 5) + tile, BF16),
            pltpu.VMEM(tile, BF16),
            pltpu.VMEM((8, 5) + tile, BF16),
            pltpu.VMEM((5,) + tile, BF16),
            pltpu.VMEM((16, 2) + tile, BF16),
            pltpu.VMEM((8, 2) + tile, BF16),
            pltpu.VMEM((4, 2) + tile, BF16),
            pltpu.VMEM((3,) + tile, BF16),
            pltpu.VMEM((4,) + tile, BF16),
            pltpu.VMEM((2, 4, 5) + tile, BF16),
            pltpu.VMEM(tile, BF16),
            pltpu.SemaphoreType.DMA((4,)),
            pltpu.SemaphoreType.DMA,
            pltpu.SemaphoreType.DMA((3,)),
            pltpu.SemaphoreType.DMA((8,)),
        ],
        compiler_params=pltpu.CompilerParams(
            collective_id=0, has_side_effects=True, vmem_limit_bytes=VMEM_BYTES
        ),
    )(*operands)
    return both[:16], both[16:]


def solution(mesh):
    return jax.shard_map(
        shards,
        mesh=mesh,
        in_specs=(P(None, "pts"), P(None, "pts"), P(None, "pts"), P(None, "pts")),
        out_specs=(P(None, "pts"), P(None, "pts")),
        check_vma=False,
    )
```

```python
import jax
import jax.numpy as jnp
from jax import lax
from jax.experimental import pallas as pl
from jax.experimental.pallas import tpu as pltpu
from jax.sharding import PartitionSpec as P

MESH = pl.DeviceIdType.MESH
F32 = jnp.float32
BF16 = jnp.bfloat16

LEAF = 256
VMEM_BYTES = 32 * 1024 * 1024
POINTS_HERE = 512
RANKS = 1600
LOW, MID, TOP67, TOP8 = 0, 320, 576, 1088

cell_units = 16.0
length_scale = 4.0
root_three = 1.7320508075688772
nugget = 0.1


def device(x, y, z, c):
    return ((x * 8 + y) * 8 + z) * 2 + c


def nt(a, b):
    return lax.dot_general(a, b, (((1,), (1,)), ((), ())), preferred_element_type=F32)


def nn(a, b):
    return jnp.dot(a, b, preferred_element_type=F32)


def send(src, dst, send_sem, recv_sem, to):
    pltpu.make_async_remote_copy(
        src_ref=src,
        dst_ref=dst,
        send_sem=send_sem,
        recv_sem=recv_sem,
        device_id=(to,),
        device_id_type=MESH,
    ).start()


def wait(ref, sem):
    pltpu.make_async_copy(ref, ref, sem).wait()


def matern(spots, leaf):
    cols = spots[:, leaf * LEAF : (leaf + 1) * LEAF]
    tall = jnp.transpose(cols)
    delta_x = tall[:, 0:1] - cols[0:1, :]
    delta_y = tall[:, 1:2] - cols[1:2, :]
    scaled = (root_three / length_scale) * jnp.sqrt(delta_x * delta_x + delta_y * delta_y)
    row = lax.broadcasted_iota(jnp.int32, (LEAF, LEAF), 0)
    col = lax.broadcasted_iota(jnp.int32, (LEAF, LEAF), 1)
    block = (1.0 + scaled) * jnp.exp(-scaled) + jnp.where(row == col, nugget, 0.0)
    return block.astype(BF16)


def kernel(
    coords_hbm, probes_hbm, u_hbm, v_hbm, out_ref,
    coords, probes, signs, w,
    give, take, snd, low0, got, mine, q8, q7, q6, q45, low_out, fin, fin0,
    load, sent, rx, rs,
):
    me = lax.axis_index("pts")
    c = me % 2
    z = (me // 2) % 8
    y = (me // 16) % 8
    x = me // 128
    core0 = c == 0
    owns = z < 4
    owns_8 = z < 2
    owns_67 = jnp.logical_and(z >= 2, z < 4)
    half = 2 - (x // 2) * 2
    beside = x + 1 - 2 * (x % 2)
    partner = device(x, y, z, 1 - c)
    v, u = w.at[0], w.at[1]
    other, own = w.at[1 - c], w.at[c]

    def chunks(n):
        return q8.at[pl.ds(0, n // 2)] if n % 2 == 0 else q8.at[pl.ds(0, n), 0]

    pieces = [(TOP8, 512), (TOP67, 512), (LOW, 576)]

    def load_bases(sources):
        for i, rows in enumerate(pieces):
            for (src, dst), sem in zip(sources, ((0, 1), (1, 2), (3, 3))[i]):
                pltpu.make_async_copy(
                    src.at[pl.ds(*rows)], dst.at[pl.ds(*rows)], load.at[sem]
                ).start()

    probes_in = pltpu.make_async_copy(probes_hbm, probes, load.at[0])
    probes_in.start()
    coords_in = pltpu.make_async_copy(coords_hbm, coords, load.at[3])

    @pl.when(core0)
    def _():
        load_bases([(u_hbm, u), (v_hbm, v)])

    @pl.when(c == 1)
    def _():
        load_bases([(v_hbm, v), (u_hbm, u)])

    coords_in.start()

    def await_rows(piece, sem):
        wait(v.at[pl.ds(*pieces[piece])], load.at[sem])

    barrier = pltpu.get_barrier_semaphore()

    def greet(to):
        pl.semaphore_signal(barrier, inc=1, device_id=(to,), device_id_type=MESH)

    greet(partner)

    @pl.when(owns)
    def _():
        for j in range(1, 8):
            greet(device(x, y, (z + j) % 8, c))

    @pl.when(owns_8)
    def _():
        for h in range(2):
            for j in range(8):
                greet(device(half + h, j, z, c))

    def siblings(n):
        node = y // n
        first = (node + 1 - 2 * (node % 2)) * n
        return [device(x, first + j, z, c) for j in range(n)]

    @pl.when(z == 1)
    def _():
        for to in siblings(1) + siblings(2):
            greet(to)

    @pl.when(z == 2)
    def _():
        for j in range(8):
            greet(device(beside, j, z, c))

    @pl.when(z == 3)
    def _():
        for to in siblings(4):
            greet(to)

    probes_in.wait()
    await_rows(0, 0)
    signs[...] = (2 * probes[...] - 1).astype(BF16)

    def coefs(bases, first, count):
        return nt(signs[...], bases[pl.ds(first, count), :])

    def lanes(part, k):
        return part[:, k * 128 : (k + 1) * 128]

    def hand_over(first, part, count, i):
        for k in range(count):
            give[first + k] = lanes(part, k)
        rows = pl.ds(first, count)
        send(give.at[rows], take.at[rows], sent, rx.at[i], partner)

    other_8 = coefs(other, TOP8, 512)

    for place, count in enumerate((20, 23, 12, 8)):
        @pl.when(z == place)
        def _():
            pl.semaphore_wait(barrier, count)

    @pl.when(jnp.logical_not(owns))
    def _():
        pl.semaphore_wait(barrier, 5)

    hand_over(0, other_8, 4, 0)
    await_rows(0, 1)
    await_rows(1, 1)
    hand_over(4, coefs(other, TOP67, 512), 4, 1)

    def to_owner(place, rows, recv_sem):
        @pl.when(z != place)
        def _():
            send(
                snd.at[place, rows], got.at[z, rows], sent, rs.at[recv_sem],
                device(x, y, place, c),
            )

        @pl.when(z == place)
        def _():
            got[place, rows] = snd[place, rows]

    own_8 = coefs(own, TOP8, 512)

    wait(take.at[pl.ds(0, 4)], rx.at[0])
    for k in range(4):
        snd[k // 2, k % 2] = (lanes(own_8, k) + take[k]).astype(BF16)
    for place in range(2):
        to_owner(place, pl.ds(0, 2), 0)

    await_rows(1, 2)
    own_67 = coefs(own, TOP67, 512)

    wait(take.at[pl.ds(4, 4)], rx.at[1])
    for k in range(4):
        snd[3 - k // 2, k % 2] = (lanes(own_67, k) + take[4 + k]).astype(BF16)
    for place in (2, 3):
        to_owner(place, pl.ds(0, 2), 0)

    coords_in.wait()
    await_rows(2, 3)
    await_rows(2, 3)
    spots = coords[...].astype(F32) / cell_units
    for leaf in range(2):
        cols = pl.ds(leaf * LEAF, LEAF)
        across = pl.ds((1 - leaf) * LEAF, LEAF)
        near = nn(signs[:, cols], matern(spots, leaf))
        coef_f = nt(signs[:, across], v[pl.ds(0, 64), across]).astype(BF16)
        coef_t = nt(signs[:, across], u[pl.ds(0, 64), across]).astype(BF16)
        out_ref[:16, cols] = near + nn(coef_f, u[pl.ds(0, 64), cols])
        out_ref[16:, cols] = near + nn(coef_t, v[pl.ds(0, 64), cols])

    other_low = coefs(other, 64, 512)
    hand_over(8, other_low, 4, 2)
    own_low = coefs(own, 64, 512)
    f_0 = jnp.where(core0, own_low[:, :64], other_low[:, :64])
    t_0 = jnp.where(core0, other_low[:, :64], own_low[:, :64])
    low0[...] = jnp.concatenate([f_0, t_0], axis=1).astype(BF16)
    send(low0, fin0, sent, rs.at[2], partner)
    wait(take.at[pl.ds(8, 4)], rx.at[2])
    for k, (place, row) in enumerate(((0, 2), (1, 2), (1, 3), (1, 4))):
        snd[place, row] = (lanes(own_low, k) + take[8 + k]).astype(BF16)
    to_owner(1, pl.ds(2, 3), 1)
    to_owner(0, pl.ds(2, 1), 1)

    def total(parts):
        return sum(part.astype(F32) for part in parts)

    @pl.when(owns)
    def _():
        wait(q8.at[pl.ds(0, 7)], rs.at[0])
        for a in range(2):
            mine[a] = total(got[k, a] for k in range(8)).astype(BF16)

    @pl.when(owns_8)
    def _():
        for j in (0, 1, 7, 2, 6, 3, 5, 4):
            for h in range(2):
                to = device(half + h, j, z, c)
                send(mine.at[pl.ds(0, 2)], q8.at[(x % 2) * 8 + y], sent, rs.at[3], to)

    @pl.when(z == 2)
    def _():
        for j in (0, 1, 7, 2, 6, 3, 5, 4):
            send(mine.at[pl.ds(0, 2)], q7.at[y], sent, rs.at[3], device(beside, j, z, c))

    @pl.when(z == 3)
    def _():
        for to in siblings(4):
            send(mine.at[pl.ds(0, 2)], q6.at[y % 4], sent, rs.at[3], to)

    def hand_out_low(own_place, source, recv_sem):
        for place in (0, 1, 2, 3, 4, 5, 6, 7):
            if place == own_place:
                fin[c, own_place, 2] = source(place)[...]
                send(source(place), fin.at[c, own_place, 2], sent, rs.at[recv_sem], partner)
            else:
                for core in range(2):
                    to = device(x, y, place, core)
                    send(source(place), fin.at[c, own_place, 2], sent, rs.at[recv_sem], to)

    @pl.when(z == 0)
    def _():
        wait(chunks(7), rs.at[1])
        hand_out_low(0, lambda place: got.at[place ^ 1, 2], 2)

    @pl.when(z == 1)
    def _():
        wait(got.at[pl.ds(0, 7), pl.ds(0, 3)], rs.at[1])
        for a in (3, 4):
            mine[a] = total(got[k, a] for k in range(8)).astype(BF16)
        for to in siblings(1):
            send(mine.at[3], q45.at[0], sent, rs.at[4], to)
        for to in siblings(2):
            send(mine.at[4], q45.at[1 + y % 2], sent, rs.at[4], to)
        pairs = [total(got[2 * k + i, 2] for i in range(2)) for k in range(4)]
        quads = [pairs[0] + pairs[1], pairs[2] + pairs[3]]
        lane = lax.broadcasted_iota(jnp.int32, (16, 128), 1)
        for k in range(4):
            low_out[k] = jnp.where(lane < 64, pairs[k ^ 1], quads[1 - k // 2]).astype(BF16)
        hand_out_low(1, lambda place: low_out.at[place // 2], 2)

    def hand_out(own_place, rows, recv_sem, places):
        src = fin.at[c, own_place, rows]
        for place in places:
            if place == own_place:
                send(src, src, sent, rs.at[recv_sem], partner)
            else:
                for core in range(2):
                    to = device(x, y, place, core)
                    send(src, src, sent, rs.at[recv_sem], to)

    @pl.when(z == 1)
    def _():
        wait(q45, rs.at[4])
        fin[c, 1, 3] = q45[0]
        fin[c, 1, 4] = total(q45[1 + k] for k in range(2)).astype(BF16)
        hand_out(1, pl.ds(3, 2), 5, range(8))

    @pl.when(z == 2)
    def _():
        wait(q7, rs.at[3])
        for a in range(2):
            fin[c, 2, a] = total(q7[k, a] for k in range(8)).astype(BF16)
        hand_out(2, pl.ds(0, 2), 6, range(6))

    @pl.when(z == 3)
    def _():
        wait(q6, rs.at[3])
        for a in range(2):
            fin[c, 3, a] = total(q6[k, a] for k in range(4)).astype(BF16)
        hand_out(3, pl.ds(0, 2), 6, range(7))

    for own_place in range(2):
        @pl.when(z == own_place)
        def _():
            wait(q8, rs.at[3])
            for a in range(2):
                fin[c, own_place, a] = total(q8[k, a] for k in range(16)).astype(BF16)
            hand_out(own_place, pl.ds(0, 2), 7, range(8 - 3 * own_place))

    def await_chunks(most, least, sem, is_own):
        @pl.when(is_own)
        def _():
            wait(chunks(least), rs.at[sem])

        @pl.when(jnp.logical_not(is_own))
        def _():
            wait(chunks(most), rs.at[sem])

    await_chunks(5, 4, 2, owns_8)
    low_f = jnp.concatenate([fin0[:, :64], fin[0, 0, 2][:, 64:], fin[0, 1, 2]], axis=1)
    low_t = jnp.concatenate([fin0[:, 64:], fin[1, 0, 2][:, 64:], fin[1, 1, 2]], axis=1)
    out_ref[:16, :] += nn(low_f, u[pl.ds(64, 256), :])
    out_ref[16:, :] += nn(low_t, v[pl.ds(64, 256), :])

    await_chunks(4, 2, 5, z == 1)

    def add(places, first):
        count = 128 * len(places)
        for kind, bases in ((0, u), (1, v)):
            coefs_here = jnp.concatenate([fin[kind, place, row] for place, row in places], axis=1)
            out_ref[kind * 16 : kind * 16 + 16, :] += nn(coefs_here, bases[pl.ds(first, count), :])

    add([(1, 3), (1, 4)], MID)

    await_chunks(8, 6, 6, owns_67)

    @pl.when(z == 1)
    def _():
        hand_out(1, pl.ds(0, 2), 7, (5, 6, 7))

    add([(3, 0), (3, 1), (2, 0), (2, 1)], TOP67)

    await_chunks(8, 6, 7, owns_8)

    add([(0, 0), (0, 1), (1, 0), (1, 1)], TOP8)

    @pl.when(z == 2)
    def _():
        hand_out(2, pl.ds(0, 2), 6, (6, 7))

    @pl.when(z == 3)
    def _():
        hand_out(3, pl.ds(0, 2), 6, (7,))

    wait(give, sent)

    def left(*sizes):
        for n in sizes:
            wait(chunks(n), sent)

    @pl.when(jnp.logical_not(owns))
    def _():
        left(13)

    @pl.when(z == 0)
    def _():
        left(10, 32, 15, 30)

    @pl.when(z == 1)
    def _():
        left(8, 32, 3, 15, 30, 30)

    @pl.when(z == 2)
    def _():
        left(11, 16, 30)

    @pl.when(z == 3)
    def _():
        left(11, 8, 30)


def shards(coords, probes, u_bases, v_bases):
    tile = (16, 128)
    operands = [
        pltpu.with_memory_space_constraint(a, pltpu.HBM) for a in (coords, probes, u_bases, v_bases)
    ]
    both = pl.pallas_call(
        kernel,
        out_shape=jax.ShapeDtypeStruct((32, POINTS_HERE), F32),
        in_specs=[pl.BlockSpec(memory_space=pl.ANY)] * 4,
        out_specs=pl.BlockSpec(memory_space=pltpu.VMEM),
        scratch_shapes=[
            pltpu.VMEM((2, POINTS_HERE), jnp.int32),
            pltpu.VMEM((16, POINTS_HERE), jnp.int32),
            pltpu.VMEM((16, POINTS_HERE), BF16),
            pltpu.VMEM((2, RANKS, POINTS_HERE), BF16),
            pltpu.VMEM((12,) + tile, F32),
            pltpu.VMEM((12,) + tile, F32),
            pltpu.VMEM((4, 5) + tile, BF16),
            pltpu.VMEM(tile, BF16),
            pltpu.VMEM((8, 5) + tile, BF16),
            pltpu.VMEM((5,) + tile, BF16),
            pltpu.VMEM((16, 2) + tile, BF16),
            pltpu.VMEM((8, 2) + tile, BF16),
            pltpu.VMEM((4, 2) + tile, BF16),
            pltpu.VMEM((3,) + tile, BF16),
            pltpu.VMEM((4,) + tile, BF16),
            pltpu.VMEM((2, 4, 5) + tile, BF16),
            pltpu.VMEM(tile, BF16),
            pltpu.SemaphoreType.DMA((4,)),
            pltpu.SemaphoreType.DMA,
            pltpu.SemaphoreType.DMA((3,)),
            pltpu.SemaphoreType.DMA((8,)),
        ],
        compiler_params=pltpu.CompilerParams(
            collective_id=0, has_side_effects=True, vmem_limit_bytes=VMEM_BYTES
        ),
    )(*operands)
    return both[:16], both[16:]


def solution(mesh):
    return jax.shard_map(
        shards,
        mesh=mesh,
        in_specs=(P(None, "pts"), P(None, "pts"), P(None, "pts"), P(None, "pts")),
        out_specs=(P(None, "pts"), P(None, "pts")),
        check_vma=False,
    )
```

```python
import jax
import jax.numpy as jnp
from jax import lax
from jax.experimental import pallas as pl
from jax.experimental.pallas import tpu as pltpu
from jax.sharding import PartitionSpec as P

MESH = pl.DeviceIdType.MESH
F32 = jnp.float32
BF16 = jnp.bfloat16

LEAF = 256
VMEM_BYTES = 32 * 1024 * 1024
POINTS_HERE = 512
RANKS = 1600
LOW, MID, TOP67, TOP8 = 0, 320, 576, 1088

cell_units = 16.0
length_scale = 4.0
root_three = 1.7320508075688772
nugget = 0.1


def device(x, y, z, c):
    return ((x * 8 + y) * 8 + z) * 2 + c


def nt(a, b):
    return lax.dot_general(a, b, (((1,), (1,)), ((), ())), preferred_element_type=F32)


def nn(a, b):
    return jnp.dot(a, b, preferred_element_type=F32)


def send(src, dst, send_sem, recv_sem, to):
    pltpu.make_async_remote_copy(
        src_ref=src,
        dst_ref=dst,
        send_sem=send_sem,
        recv_sem=recv_sem,
        device_id=(to,),
        device_id_type=MESH,
    ).start()


def wait(ref, sem):
    pltpu.make_async_copy(ref, ref, sem).wait()


def matern(spots, leaf):
    cols = spots[:, leaf * LEAF : (leaf + 1) * LEAF]
    tall = jnp.transpose(cols)
    delta_x = tall[:, 0:1] - cols[0:1, :]
    delta_y = tall[:, 1:2] - cols[1:2, :]
    scaled = (root_three / length_scale) * jnp.sqrt(delta_x * delta_x + delta_y * delta_y)
    row = lax.broadcasted_iota(jnp.int32, (LEAF, LEAF), 0)
    col = lax.broadcasted_iota(jnp.int32, (LEAF, LEAF), 1)
    block = (1.0 + scaled) * jnp.exp(-scaled) + jnp.where(row == col, nugget, 0.0)
    return block.astype(BF16)


def kernel(
    coords_hbm, probes_hbm, u_hbm, v_hbm, out_ref,
    coords, probes, signs, w,
    give, take, snd, low0, got, mine, q8, q7, q6, q45, low_out, fin, fin0,
    load, sent, rx, rs,
):
    me = lax.axis_index("pts")
    c = me % 2
    z = (me // 2) % 8
    y = (me // 16) % 8
    x = me // 128
    core0 = c == 0
    owns = z < 4
    owns_8 = z < 2
    owns_67 = jnp.logical_and(z >= 2, z < 4)
    half = 2 - (x // 2) * 2
    beside = x + 1 - 2 * (x % 2)
    partner = device(x, y, z, 1 - c)
    v, u = w.at[0], w.at[1]
    other, own = w.at[1 - c], w.at[c]

    def chunks(n):
        return q8.at[pl.ds(0, n // 2)] if n % 2 == 0 else q8.at[pl.ds(0, n), 0]

    pieces = [(TOP8, 512), (TOP67, 512), (LOW, 576)]

    def load_bases(sources):
        for i, rows in enumerate(pieces):
            for (src, dst), sem in zip(sources, ((0, 1), (1, 2), (3, 3))[i]):
                pltpu.make_async_copy(
                    src.at[pl.ds(*rows)], dst.at[pl.ds(*rows)], load.at[sem]
                ).start()

    probes_in = pltpu.make_async_copy(probes_hbm, probes, load.at[0])
    probes_in.start()
    coords_in = pltpu.make_async_copy(coords_hbm, coords, load.at[3])

    @pl.when(core0)
    def _():
        load_bases([(u_hbm, u), (v_hbm, v)])

    @pl.when(c == 1)
    def _():
        load_bases([(v_hbm, v), (u_hbm, u)])

    coords_in.start()

    def await_rows(piece, sem):
        wait(v.at[pl.ds(*pieces[piece])], load.at[sem])

    barrier = pltpu.get_barrier_semaphore()

    def greet(to):
        pl.semaphore_signal(barrier, inc=1, device_id=(to,), device_id_type=MESH)

    greet(partner)

    @pl.when(owns)
    def _():
        for j in range(1, 8):
            greet(device(x, y, (z + j) % 8, c))

    @pl.when(owns_8)
    def _():
        for h in range(2):
            for j in range(8):
                greet(device(half + h, j, z, c))

    def siblings(n):
        node = y // n
        first = (node + 1 - 2 * (node % 2)) * n
        return [device(x, first + j, z, c) for j in range(n)]

    @pl.when(z == 1)
    def _():
        for to in siblings(1) + siblings(2):
            greet(to)

    @pl.when(z == 2)
    def _():
        for j in range(8):
            greet(device(beside, j, z, c))

    @pl.when(z == 3)
    def _():
        for to in siblings(4):
            greet(to)

    probes_in.wait()
    await_rows(0, 0)
    signs[...] = (2 * probes[...] - 1).astype(BF16)

    def coefs(bases, first, count):
        return nt(signs[...], bases[pl.ds(first, count), :])

    def lanes(part, k):
        return part[:, k * 128 : (k + 1) * 128]

    def hand_over(first, part, count, i):
        for k in range(count):
            give[first + k] = lanes(part, k)
        rows = pl.ds(first, count)
        send(give.at[rows], take.at[rows], sent, rx.at[i], partner)

    other_8 = coefs(other, TOP8 + 256, 256)

    for place, count in enumerate((20, 23, 12, 8)):
        @pl.when(z == place)
        def _():
            pl.semaphore_wait(barrier, count)

    @pl.when(jnp.logical_not(owns))
    def _():
        pl.semaphore_wait(barrier, 5)

    hand_over(2, other_8, 2, 0)
    hand_over(0, coefs(other, TOP8, 256), 2, 3)
    await_rows(0, 1)
    await_rows(1, 1)
    hand_over(4, coefs(other, TOP67, 512), 4, 1)

    def to_owner(place, rows, recv_sem):
        @pl.when(z != place)
        def _():
            send(
                snd.at[place, rows], got.at[z, rows], sent, rs.at[recv_sem],
                device(x, y, place, c),
            )

        @pl.when(z == place)
        def _():
            got[place, rows] = snd[place, rows]

    for place, i in ((1, 0), (0, 3)):
        own_8 = coefs(own, TOP8 + 256 * place, 256)
        wait(take.at[pl.ds(2 * place, 2)], rx.at[i])
        for k in range(2):
            snd[place, k] = (lanes(own_8, k) + take[2 * place + k]).astype(BF16)
        to_owner(place, pl.ds(0, 2), 0)

    await_rows(1, 2)
    own_67 = coefs(own, TOP67, 512)

    wait(take.at[pl.ds(4, 4)], rx.at[1])
    for k in range(4):
        snd[3 - k // 2, k % 2] = (lanes(own_67, k) + take[4 + k]).astype(BF16)
    for place in (2, 3):
        to_owner(place, pl.ds(0, 2), 0)

    coords_in.wait()
    await_rows(2, 3)
    await_rows(2, 3)
    spots = coords[...].astype(F32) / cell_units
    for leaf in range(2):
        cols = pl.ds(leaf * LEAF, LEAF)
        across = pl.ds((1 - leaf) * LEAF, LEAF)
        near = nn(signs[:, cols], matern(spots, leaf))
        coef_f = nt(signs[:, across], v[pl.ds(0, 64), across]).astype(BF16)
        coef_t = nt(signs[:, across], u[pl.ds(0, 64), across]).astype(BF16)
        out_ref[:16, cols] = near + nn(coef_f, u[pl.ds(0, 64), cols])
        out_ref[16:, cols] = near + nn(coef_t, v[pl.ds(0, 64), cols])

    other_low = coefs(other, 64, 512)
    hand_over(8, other_low, 4, 2)
    own_low = coefs(own, 64, 512)
    f_0 = jnp.where(core0, own_low[:, :64], other_low[:, :64])
    t_0 = jnp.where(core0, other_low[:, :64], own_low[:, :64])
    low0[...] = jnp.concatenate([f_0, t_0], axis=1).astype(BF16)
    send(low0, fin0, sent, rs.at[2], partner)
    wait(take.at[pl.ds(8, 4)], rx.at[2])
    for k, (place, row) in enumerate(((0, 2), (1, 2), (1, 3), (1, 4))):
        snd[place, row] = (lanes(own_low, k) + take[8 + k]).astype(BF16)
    to_owner(1, pl.ds(2, 3), 1)
    to_owner(0, pl.ds(2, 1), 1)

    def total(parts):
        return sum(part.astype(F32) for part in parts)

    @pl.when(owns)
    def _():
        wait(q8.at[pl.ds(0, 7)], rs.at[0])
        for a in range(2):
            mine[a] = total(got[k, a] for k in range(8)).astype(BF16)

    @pl.when(owns_8)
    def _():
        for j in (0, 1, 7, 2, 6, 3, 5, 4):
            for h in range(2):
                to = device(half + h, j, z, c)
                send(mine.at[pl.ds(0, 2)], q8.at[(x % 2) * 8 + y], sent, rs.at[3], to)

    @pl.when(z == 2)
    def _():
        for j in (0, 1, 7, 2, 6, 3, 5, 4):
            send(mine.at[pl.ds(0, 2)], q7.at[y], sent, rs.at[3], device(beside, j, z, c))

    @pl.when(z == 3)
    def _():
        for to in siblings(4):
            send(mine.at[pl.ds(0, 2)], q6.at[y % 4], sent, rs.at[3], to)

    def hand_out_low(own_place, source, recv_sem):
        for place in (0, 1, 2, 3, 4, 5, 6, 7):
            if place == own_place:
                fin[c, own_place, 2] = source(place)[...]
                send(source(place), fin.at[c, own_place, 2], sent, rs.at[recv_sem], partner)
            else:
                for core in (1, 0):
                    to = device(x, y, place, core)
                    send(source(place), fin.at[c, own_place, 2], sent, rs.at[recv_sem], to)

    @pl.when(z == 0)
    def _():
        wait(chunks(7), rs.at[1])
        hand_out_low(0, lambda place: got.at[place ^ 1, 2], 2)

    @pl.when(z == 1)
    def _():
        wait(got.at[pl.ds(0, 7), pl.ds(0, 3)], rs.at[1])
        for a in (3, 4):
            mine[a] = total(got[k, a] for k in range(8)).astype(BF16)
        for to in siblings(1):
            send(mine.at[3], q45.at[0], sent, rs.at[4], to)
        for to in siblings(2):
            send(mine.at[4], q45.at[1 + y % 2], sent, rs.at[4], to)
        pairs = [total(got[2 * k + i, 2] for i in range(2)) for k in range(4)]
        quads = [pairs[0] + pairs[1], pairs[2] + pairs[3]]
        lane = lax.broadcasted_iota(jnp.int32, (16, 128), 1)
        for k in range(4):
            low_out[k] = jnp.where(lane < 64, pairs[k ^ 1], quads[1 - k // 2]).astype(BF16)
        hand_out_low(1, lambda place: low_out.at[place // 2], 2)

    def hand_out(own_place, rows, recv_sem, places):
        src = fin.at[c, own_place, rows]
        for place in places:
            if place == own_place:
                send(src, src, sent, rs.at[recv_sem], partner)
            else:
                for core in (1, 0):
                    to = device(x, y, place, core)
                    send(src, src, sent, rs.at[recv_sem], to)

    @pl.when(z == 1)
    def _():
        wait(q45, rs.at[4])
        fin[c, 1, 3] = q45[0]
        fin[c, 1, 4] = total(q45[1 + k] for k in range(2)).astype(BF16)
        hand_out(1, pl.ds(3, 2), 5, range(8))

    @pl.when(z == 2)
    def _():
        wait(q7, rs.at[3])
        for a in range(2):
            fin[c, 2, a] = total(q7[k, a] for k in range(8)).astype(BF16)
        hand_out(2, pl.ds(0, 2), 6, range(6))

    @pl.when(z == 3)
    def _():
        wait(q6, rs.at[3])
        for a in range(2):
            fin[c, 3, a] = total(q6[k, a] for k in range(4)).astype(BF16)
        hand_out(3, pl.ds(0, 2), 6, range(7))

    for own_place in range(2):
        @pl.when(z == own_place)
        def _():
            wait(q8, rs.at[3])
            for a in range(2):
                fin[c, own_place, a] = total(q8[k, a] for k in range(16)).astype(BF16)
            hand_out(own_place, pl.ds(0, 2), 7 + own_place, range(8 - 3 * own_place))

    def await_chunks(most, least, sem, is_own):
        @pl.when(is_own)
        def _():
            wait(chunks(least), rs.at[sem])

        @pl.when(jnp.logical_not(is_own))
        def _():
            wait(chunks(most), rs.at[sem])

    await_chunks(5, 4, 2, owns_8)
    low_f = jnp.concatenate([fin0[:, :64], fin[0, 0, 2][:, 64:], fin[0, 1, 2]], axis=1)
    low_t = jnp.concatenate([fin0[:, 64:], fin[1, 0, 2][:, 64:], fin[1, 1, 2]], axis=1)
    out_ref[:16, :] += nn(low_f, u[pl.ds(64, 256), :])
    out_ref[16:, :] += nn(low_t, v[pl.ds(64, 256), :])

    await_chunks(4, 2, 5, z == 1)

    def add(places, first):
        count = 128 * len(places)
        for kind, bases in ((0, u), (1, v)):
            coefs_here = jnp.concatenate([fin[kind, place, row] for place, row in places], axis=1)
            out_ref[kind * 16 : kind * 16 + 16, :] += nn(coefs_here, bases[pl.ds(first, count), :])

    add([(1, 3), (1, 4)], MID)

    await_chunks(8, 6, 6, owns_67)

    @pl.when(z == 1)
    def _():
        hand_out(1, pl.ds(0, 2), 8, (5, 6, 7))

    add([(3, 0), (3, 1), (2, 0), (2, 1)], TOP67)

    for place in range(2):
        await_chunks(4, 2, 7 + place, z == place)
        add([(place, 0), (place, 1)], TOP8 + 256 * place)

    @pl.when(z == 2)
    def _():
        hand_out(2, pl.ds(0, 2), 6, (6, 7))

    @pl.when(z == 3)
    def _():
        hand_out(3, pl.ds(0, 2), 6, (7,))

    wait(give, sent)

    def left(*sizes):
        for n in sizes:
            wait(chunks(n), sent)

    @pl.when(jnp.logical_not(owns))
    def _():
        left(13)

    @pl.when(z == 0)
    def _():
        left(10, 32, 15, 30)

    @pl.when(z == 1)
    def _():
        left(8, 32, 3, 15, 30, 30)

    @pl.when(z == 2)
    def _():
        left(11, 16, 30)

    @pl.when(z == 3)
    def _():
        left(11, 8, 30)


def shards(coords, probes, u_bases, v_bases):
    tile = (16, 128)
    operands = [
        pltpu.with_memory_space_constraint(a, pltpu.HBM) for a in (coords, probes, u_bases, v_bases)
    ]
    both = pl.pallas_call(
        kernel,
        out_shape=jax.ShapeDtypeStruct((32, POINTS_HERE), F32),
        in_specs=[pl.BlockSpec(memory_space=pl.ANY)] * 4,
        out_specs=pl.BlockSpec(memory_space=pltpu.VMEM),
        scratch_shapes=[
            pltpu.VMEM((2, POINTS_HERE), jnp.int32),
            pltpu.VMEM((16, POINTS_HERE), jnp.int32),
            pltpu.VMEM((16, POINTS_HERE), BF16),
            pltpu.VMEM((2, RANKS, POINTS_HERE), BF16),
            pltpu.VMEM((12,) + tile, F32),
            pltpu.VMEM((12,) + tile, F32),
            pltpu.VMEM((4, 5) + tile, BF16),
            pltpu.VMEM(tile, BF16),
            pltpu.VMEM((8, 5) + tile, BF16),
            pltpu.VMEM((5,) + tile, BF16),
            pltpu.VMEM((16, 2) + tile, BF16),
            pltpu.VMEM((8, 2) + tile, BF16),
            pltpu.VMEM((4, 2) + tile, BF16),
            pltpu.VMEM((3,) + tile, BF16),
            pltpu.VMEM((4,) + tile, BF16),
            pltpu.VMEM((2, 4, 5) + tile, BF16),
            pltpu.VMEM(tile, BF16),
            pltpu.SemaphoreType.DMA((4,)),
            pltpu.SemaphoreType.DMA,
            pltpu.SemaphoreType.DMA((4,)),
            pltpu.SemaphoreType.DMA((9,)),
        ],
        compiler_params=pltpu.CompilerParams(
            collective_id=0, has_side_effects=True, vmem_limit_bytes=VMEM_BYTES
        ),
    )(*operands)
    return both[:16], both[16:]


def solution(mesh):
    return jax.shard_map(
        shards,
        mesh=mesh,
        in_specs=(P(None, "pts"), P(None, "pts"), P(None, "pts"), P(None, "pts")),
        out_specs=(P(None, "pts"), P(None, "pts")),
        check_vma=False,
    )
```

```python
import jax
import jax.numpy as jnp
from jax import lax
from jax.experimental import pallas as pl
from jax.experimental.pallas import tpu as pltpu
from jax.sharding import PartitionSpec as P

MESH = pl.DeviceIdType.MESH
F32 = jnp.float32
BF16 = jnp.bfloat16

LEAF = 256
VMEM_BYTES = 32 * 1024 * 1024
POINTS_HERE = 512
RANKS = 1600
LOW, MID, TOP67, TOP8 = 0, 320, 576, 1088

cell_units = 16.0
length_scale = 4.0
root_three = 1.7320508075688772
nugget = 0.1


def device(x, y, z, c):
    return ((x * 8 + y) * 8 + z) * 2 + c


def nt(a, b):
    return lax.dot_general(a, b, (((1,), (1,)), ((), ())), preferred_element_type=F32)


def nn(a, b):
    return jnp.dot(a, b, preferred_element_type=F32)


def send(src, dst, send_sem, recv_sem, to):
    pltpu.make_async_remote_copy(
        src_ref=src,
        dst_ref=dst,
        send_sem=send_sem,
        recv_sem=recv_sem,
        device_id=(to,),
        device_id_type=MESH,
    ).start()


def wait(ref, sem):
    pltpu.make_async_copy(ref, ref, sem).wait()


def matern(spots, leaf):
    cols = spots[:, leaf * LEAF : (leaf + 1) * LEAF]
    tall = jnp.transpose(cols)
    delta_x = tall[:, 0:1] - cols[0:1, :]
    delta_y = tall[:, 1:2] - cols[1:2, :]
    scaled = (root_three / length_scale) * jnp.sqrt(delta_x * delta_x + delta_y * delta_y)
    row = lax.broadcasted_iota(jnp.int32, (LEAF, LEAF), 0)
    col = lax.broadcasted_iota(jnp.int32, (LEAF, LEAF), 1)
    block = (1.0 + scaled) * jnp.exp(-scaled) + jnp.where(row == col, nugget, 0.0)
    return block.astype(BF16)


def kernel(
    coords_hbm, probes_hbm, u_hbm, v_hbm, out_ref,
    coords, probes, signs, w,
    give, take, snd, low0, got, mine, q8, q7, q6, q45, low_out, fin, fin0,
    load, sent, rx, rs,
):
    me = lax.axis_index("pts")
    c = me % 2
    z = (me // 2) % 8
    y = (me // 16) % 8
    x = me // 128
    core0 = c == 0
    core1 = c == 1
    zc = z * 2 + c
    owns = jnp.logical_and(core1, z < 4)
    owns_8 = jnp.logical_and(core1, z < 2)
    owns_67 = jnp.logical_and(owns, z >= 2)

    def at(place):
        return jnp.logical_and(core1, z == place)

    half = 2 - (x // 2) * 2
    beside = x + 1 - 2 * (x % 2)
    partner = device(x, y, z, 1 - c)
    v, u = w.at[0], w.at[1]
    other, own = w.at[1 - c], w.at[c]

    def chunks(n):
        if n % 4 == 0:
            return q8.at[pl.ds(0, n // 4)]
        return q8.at[pl.ds(0, n // 2), 0] if n % 2 == 0 else q8.at[pl.ds(0, n), 0, 0]

    pieces = [(TOP8, 512), (TOP67, 512), (LOW, 576)]

    def load_bases(sources):
        for i, rows in enumerate(pieces):
            for (src, dst), sem in zip(sources, ((0, 1), (1, 2), (3, 3))[i]):
                pltpu.make_async_copy(
                    src.at[pl.ds(*rows)], dst.at[pl.ds(*rows)], load.at[sem]
                ).start()

    probes_in = pltpu.make_async_copy(probes_hbm, probes, load.at[0])
    probes_in.start()
    coords_in = pltpu.make_async_copy(coords_hbm, coords, load.at[3])

    @pl.when(core0)
    def _():
        load_bases([(u_hbm, u), (v_hbm, v)])

    @pl.when(c == 1)
    def _():
        load_bases([(v_hbm, v), (u_hbm, u)])

    coords_in.start()

    def await_rows(piece, sem):
        wait(v.at[pl.ds(*pieces[piece])], load.at[sem])

    barrier = pltpu.get_barrier_semaphore()

    def greet(to):
        pl.semaphore_signal(barrier, inc=1, device_id=(to,), device_id_type=MESH)

    greet(partner)

    @pl.when(owns)
    def _():
        for j in range(1, 16):
            o = (zc + j) % 16
            greet(device(x, y, o // 2, o % 2))

    @pl.when(owns_8)
    def _():
        for h in range(2):
            for j in range(8):
                greet(device(half + h, j, z, c))

    def siblings(n):
        node = y // n
        first = (node + 1 - 2 * (node % 2)) * n
        return [device(x, first + j, z, c) for j in range(n)]

    @pl.when(at(1))
    def _():
        for to in siblings(1) + siblings(2):
            greet(to)

    @pl.when(at(2))
    def _():
        for j in range(8):
            greet(device(beside, j, z, c))

    @pl.when(at(3))
    def _():
        for to in siblings(4):
            greet(to)

    probes_in.wait()
    await_rows(0, 0)
    signs[...] = (2 * probes[...] - 1).astype(BF16)

    def coefs(bases, first, count):
        return nt(signs[...], bases[pl.ds(first, count), :])

    def lanes(part, k):
        return part[:, k * 128 : (k + 1) * 128]

    def hand_over(first, part, count, i):
        for k in range(count):
            give[first + k] = lanes(part, k)
        rows = pl.ds(first, count)
        send(give.at[rows], take.at[rows], sent, rx.at[i], partner)

    other_8 = coefs(other, TOP8 + 256, 256)

    for place, count in enumerate((20, 23, 12, 8)):
        @pl.when(at(place))
        def _():
            pl.semaphore_wait(barrier, count)

    @pl.when(jnp.logical_not(owns))
    def _():
        pl.semaphore_wait(barrier, 5)

    hand_over(2, other_8, 2, 0)
    hand_over(0, coefs(other, TOP8, 256), 2, 3)
    await_rows(0, 1)
    await_rows(1, 1)
    hand_over(4, coefs(other, TOP67, 512), 4, 1)

    def to_owner(place, rows, recv_sem):
        @pl.when(jnp.logical_not(at(place)))
        def _():
            send(
                snd.at[place, rows], got.at[z, rows, c], sent, rs.at[recv_sem],
                device(x, y, place, 1),
            )

        @pl.when(at(place))
        def _():
            got[place, rows, 1] = snd[place, rows]

    for place, i in ((1, 0), (0, 3)):
        own_8 = coefs(own, TOP8 + 256 * place, 256)
        wait(take.at[pl.ds(2 * place, 2)], rx.at[i])
        for k in range(2):
            snd[place, k] = (lanes(own_8, k) + take[2 * place + k]).astype(BF16)
        to_owner(place, pl.ds(0, 2), 0)

    await_rows(1, 2)
    own_67 = coefs(own, TOP67, 512)

    wait(take.at[pl.ds(4, 4)], rx.at[1])
    for k in range(4):
        snd[3 - k // 2, k % 2] = (lanes(own_67, k) + take[4 + k]).astype(BF16)
    for place in (2, 3):
        to_owner(place, pl.ds(0, 2), 0)

    coords_in.wait()
    await_rows(2, 3)
    await_rows(2, 3)
    spots = coords[...].astype(F32) / cell_units
    for leaf in range(2):
        cols = pl.ds(leaf * LEAF, LEAF)
        across = pl.ds((1 - leaf) * LEAF, LEAF)
        near = nn(signs[:, cols], matern(spots, leaf))
        coef_f = nt(signs[:, across], v[pl.ds(0, 64), across]).astype(BF16)
        coef_t = nt(signs[:, across], u[pl.ds(0, 64), across]).astype(BF16)
        out_ref[:16, cols] = near + nn(coef_f, u[pl.ds(0, 64), cols])
        out_ref[16:, cols] = near + nn(coef_t, v[pl.ds(0, 64), cols])

    other_low = coefs(other, 64, 512)
    hand_over(8, other_low, 4, 2)
    own_low = coefs(own, 64, 512)
    f_0 = jnp.where(core0, own_low[:, :64], other_low[:, :64])
    t_0 = jnp.where(core0, other_low[:, :64], own_low[:, :64])
    low0[...] = jnp.concatenate([f_0, t_0], axis=1).astype(BF16)
    send(low0, fin0, sent, rs.at[2], partner)
    wait(take.at[pl.ds(8, 4)], rx.at[2])
    for k, (place, row) in enumerate(((0, 2), (1, 2), (1, 3), (1, 4))):
        snd[place, row] = (lanes(own_low, k) + take[8 + k]).astype(BF16)
    to_owner(1, pl.ds(3, 2), 1)
    to_owner(1, pl.ds(2, 1), 9)
    to_owner(0, pl.ds(2, 1), 1)

    def total(parts):
        return sum(part.astype(F32) for part in parts)

    def add_up(into, row, parts):
        for kind in range(2):
            into[row, kind] = total(part[kind] for part in parts).astype(BF16)

    @pl.when(owns)
    def _():
        wait(chunks(30), rs.at[0])
        for a in range(2):
            add_up(mine, a, [got.at[k, a] for k in range(8)])

    @pl.when(owns_8)
    def _():
        for j in (0, 1, 7, 2, 6, 3, 5, 4):
            for h in range(2):
                to = device(half + h, j, z, c)
                send(mine.at[pl.ds(0, 2)], q8.at[(x % 2) * 8 + y], sent, rs.at[3], to)

    @pl.when(at(2))
    def _():
        for j in (0, 1, 7, 2, 6, 3, 5, 4):
            send(mine.at[pl.ds(0, 2)], q7.at[y], sent, rs.at[3], device(beside, j, z, c))

    @pl.when(at(3))
    def _():
        for to in siblings(4):
            send(mine.at[pl.ds(0, 2)], q6.at[y % 4], sent, rs.at[3], to)

    def hand_out_low(own_place, source, recv_sem):
        for place in (0, 1, 2, 3, 4, 5, 6, 7):
            if place == own_place:
                fin[own_place, 2] = source(place)[...]
                send(source(place), fin.at[own_place, 2], sent, rs.at[recv_sem], partner)
            else:
                for core in (1, 0):
                    to = device(x, y, place, core)
                    send(source(place), fin.at[own_place, 2], sent, rs.at[recv_sem], to)

    @pl.when(at(0))
    def _():
        wait(chunks(15), rs.at[1])
        hand_out_low(0, lambda place: got.at[place ^ 1, 2], 2)

    @pl.when(at(1))
    def _():
        wait(chunks(30), rs.at[1])
        wait(chunks(15), rs.at[9])
        for a in (3, 4):
            add_up(mine, a, [got.at[k, a] for k in range(8)])
        for to in siblings(1):
            send(mine.at[3], q45.at[0], sent, rs.at[4], to)
        for to in siblings(2):
            send(mine.at[4], q45.at[1 + y % 2], sent, rs.at[4], to)
        lane = lax.broadcasted_iota(jnp.int32, (16, 128), 1)
        for kind in range(2):
            pairs = [total(got[2 * k + i, 2, kind] for i in range(2)) for k in range(4)]
            quads = [pairs[0] + pairs[1], pairs[2] + pairs[3]]
            for k in range(4):
                low_out[k, kind] = jnp.where(lane < 64, pairs[k ^ 1], quads[1 - k // 2]).astype(BF16)
        hand_out_low(1, lambda place: low_out.at[place // 2], 2)

    def hand_out(own_place, rows, recv_sem, places):
        src = fin.at[own_place, rows]
        for place in places:
            if place == own_place:
                send(src, src, sent, rs.at[recv_sem], partner)
            else:
                for core in (1, 0):
                    to = device(x, y, place, core)
                    send(src, src, sent, rs.at[recv_sem], to)

    @pl.when(at(1))
    def _():
        wait(q45, rs.at[4])
        fin[1, 3] = q45[0]
        add_up(fin.at[1], 4, [q45.at[1 + k] for k in range(2)])
        hand_out(1, pl.ds(3, 2), 5, range(8))

    @pl.when(at(2))
    def _():
        wait(q7, rs.at[3])
        for a in range(2):
            add_up(fin.at[2], a, [q7.at[k, a] for k in range(8)])
        hand_out(2, pl.ds(0, 2), 6, range(6))

    @pl.when(at(3))
    def _():
        wait(q6, rs.at[3])
        for a in range(2):
            add_up(fin.at[3], a, [q6.at[k, a] for k in range(4)])
        hand_out(3, pl.ds(0, 2), 6, range(7))

    for own_place in range(2):
        @pl.when(at(own_place))
        def _():
            wait(q8, rs.at[3])
            for a in range(2):
                add_up(fin.at[own_place], a, [q8.at[k, a] for k in range(16)])
            hand_out(own_place, pl.ds(0, 2), 7 + own_place, range(8 - 3 * own_place))

    def await_chunks(most, least, sem, is_own):
        if least:
            @pl.when(is_own)
            def _():
                wait(chunks(least), rs.at[sem])

        @pl.when(jnp.logical_not(is_own))
        def _():
            wait(chunks(most), rs.at[sem])

    await_chunks(5, 3, 2, owns_8)
    low_f = jnp.concatenate([fin0[:, :64], fin[0, 2, 0][:, 64:], fin[1, 2, 0]], axis=1)
    low_t = jnp.concatenate([fin0[:, 64:], fin[0, 2, 1][:, 64:], fin[1, 2, 1]], axis=1)
    out_ref[:16, :] += nn(low_f, u[pl.ds(64, 256), :])
    out_ref[16:, :] += nn(low_t, v[pl.ds(64, 256), :])

    await_chunks(4, 0, 5, at(1))

    def add(places, first):
        count = 128 * len(places)
        for kind, bases in ((0, u), (1, v)):
            coefs_here = jnp.concatenate([fin[place, row, kind] for place, row in places], axis=1)
            out_ref[kind * 16 : kind * 16 + 16, :] += nn(coefs_here, bases[pl.ds(first, count), :])

    add([(1, 3), (1, 4)], MID)

    await_chunks(8, 4, 6, owns_67)

    @pl.when(at(1))
    def _():
        hand_out(1, pl.ds(0, 2), 8, (5, 6, 7))

    add([(3, 0), (3, 1), (2, 0), (2, 1)], TOP67)

    for place in range(2):
        await_chunks(4, 0, 7 + place, at(place))
        add([(place, 0), (place, 1)], TOP8 + 256 * place)

    @pl.when(at(2))
    def _():
        hand_out(2, pl.ds(0, 2), 6, (6, 7))

    @pl.when(at(3))
    def _():
        hand_out(3, pl.ds(0, 2), 6, (7,))

    wait(give, sent)

    def left(*sizes):
        for n in sizes:
            wait(chunks(n), sent)

    @pl.when(jnp.logical_not(owns))
    def _():
        left(13)

    @pl.when(at(0))
    def _():
        left(10, 64, 30, 60)

    @pl.when(at(1))
    def _():
        left(8, 64, 6, 30, 60, 60)

    @pl.when(at(2))
    def _():
        left(11, 32, 60)

    @pl.when(at(3))
    def _():
        left(11, 16, 60)


def shards(coords, probes, u_bases, v_bases):
    tile = (16, 128)
    operands = [
        pltpu.with_memory_space_constraint(a, pltpu.HBM) for a in (coords, probes, u_bases, v_bases)
    ]
    both = pl.pallas_call(
        kernel,
        out_shape=jax.ShapeDtypeStruct((32, POINTS_HERE), F32),
        in_specs=[pl.BlockSpec(memory_space=pl.ANY)] * 4,
        out_specs=pl.BlockSpec(memory_space=pltpu.VMEM),
        scratch_shapes=[
            pltpu.VMEM((2, POINTS_HERE), jnp.int32),
            pltpu.VMEM((16, POINTS_HERE), jnp.int32),
            pltpu.VMEM((16, POINTS_HERE), BF16),
            pltpu.VMEM((2, RANKS, POINTS_HERE), BF16),
            pltpu.VMEM((12,) + tile, F32),
            pltpu.VMEM((12,) + tile, F32),
            pltpu.VMEM((4, 5) + tile, BF16),
            pltpu.VMEM(tile, BF16),
            pltpu.VMEM((8, 5, 2) + tile, BF16),
            pltpu.VMEM((5, 2) + tile, BF16),
            pltpu.VMEM((16, 2, 2) + tile, BF16),
            pltpu.VMEM((8, 2, 2) + tile, BF16),
            pltpu.VMEM((4, 2, 2) + tile, BF16),
            pltpu.VMEM((3, 2) + tile, BF16),
            pltpu.VMEM((4, 2) + tile, BF16),
            pltpu.VMEM((4, 5, 2) + tile, BF16),
            pltpu.VMEM(tile, BF16),
            pltpu.SemaphoreType.DMA((4,)),
            pltpu.SemaphoreType.DMA,
            pltpu.SemaphoreType.DMA((4,)),
            pltpu.SemaphoreType.DMA((10,)),
        ],
        compiler_params=pltpu.CompilerParams(
            collective_id=0, has_side_effects=True, vmem_limit_bytes=VMEM_BYTES
        ),
    )(*operands)
    return both[:16], both[16:]


def solution(mesh):
    return jax.shard_map(
        shards,
        mesh=mesh,
        in_specs=(P(None, "pts"), P(None, "pts"), P(None, "pts"), P(None, "pts")),
        out_specs=(P(None, "pts"), P(None, "pts")),
        check_vma=False,
    )
```

```python
import jax
import jax.numpy as jnp
from jax import lax
from jax.experimental import pallas as pl
from jax.experimental.pallas import tpu as pltpu
from jax.sharding import PartitionSpec as P

MESH = pl.DeviceIdType.MESH
F32 = jnp.float32
BF16 = jnp.bfloat16

LEAF = 256
VMEM_BYTES = 32 * 1024 * 1024
POINTS_HERE = 512
RANKS = 1600
LOW, MID, TOP67, TOP8 = 0, 320, 576, 1088

cell_units = 16.0
length_scale = 4.0
root_three = 1.7320508075688772
nugget = 0.1


def device(x, y, z, c):
    return ((x * 8 + y) * 8 + z) * 2 + c


def nt(a, b):
    return lax.dot_general(a, b, (((1,), (1,)), ((), ())), preferred_element_type=F32)


def nn(a, b):
    return jnp.dot(a, b, preferred_element_type=F32)


def send(src, dst, send_sem, recv_sem, to):
    pltpu.make_async_remote_copy(
        src_ref=src,
        dst_ref=dst,
        send_sem=send_sem,
        recv_sem=recv_sem,
        device_id=(to,),
        device_id_type=MESH,
    ).start()


def wait(ref, sem):
    pltpu.make_async_copy(ref, ref, sem).wait()


def matern(spots, leaf):
    cols = spots[:, leaf * LEAF : (leaf + 1) * LEAF]
    tall = jnp.transpose(cols)
    delta_x = tall[:, 0:1] - cols[0:1, :]
    delta_y = tall[:, 1:2] - cols[1:2, :]
    scaled = (root_three / length_scale) * jnp.sqrt(delta_x * delta_x + delta_y * delta_y)
    row = lax.broadcasted_iota(jnp.int32, (LEAF, LEAF), 0)
    col = lax.broadcasted_iota(jnp.int32, (LEAF, LEAF), 1)
    block = (1.0 + scaled) * jnp.exp(-scaled) + jnp.where(row == col, nugget, 0.0)
    return block.astype(BF16)


def kernel(
    coords_hbm, probes_hbm, u_hbm, v_hbm, out_ref,
    coords, probes, signs, w,
    give, take, snd, low0, got, mine, q8, q7, q6, q45, low_out, fin, fin0,
    load, sent, rx, rs,
):
    me = lax.axis_index("pts")
    c = me % 2
    z = (me // 2) % 8
    y = (me // 16) % 8
    x = me // 128
    core0 = c == 0
    core1 = c == 1
    zc = z * 2 + c
    owns = jnp.logical_and(core1, z < 4)
    owns_8 = jnp.logical_and(core1, z < 2)
    owns_67 = jnp.logical_and(owns, z >= 2)

    def at(place):
        return jnp.logical_and(core1, z == place)

    half = 2 - (x // 2) * 2
    beside = x + 1 - 2 * (x % 2)
    partner = device(x, y, z, 1 - c)
    v, u = w.at[0], w.at[1]
    other, own = w.at[1 - c], w.at[c]

    def chunks(n):
        if n % 4 == 0:
            return q8.at[pl.ds(0, n // 4)]
        return q8.at[pl.ds(0, n // 2), 0] if n % 2 == 0 else q8.at[pl.ds(0, n), 0, 0]

    pieces = [(TOP8, 512), (TOP67, 512), (LOW, 576)]

    def load_bases(sources):
        for i, rows in enumerate(pieces):
            for (src, dst), sem in zip(sources, ((0, 1), (1, 2), (3, 3))[i]):
                pltpu.make_async_copy(
                    src.at[pl.ds(*rows)], dst.at[pl.ds(*rows)], load.at[sem]
                ).start()

    probes_in = pltpu.make_async_copy(probes_hbm, probes, load.at[0])
    probes_in.start()
    coords_in = pltpu.make_async_copy(coords_hbm, coords, load.at[3])

    @pl.when(core0)
    def _():
        load_bases([(u_hbm, u), (v_hbm, v)])

    @pl.when(c == 1)
    def _():
        load_bases([(v_hbm, v), (u_hbm, u)])

    coords_in.start()

    def await_rows(piece, sem):
        wait(v.at[pl.ds(*pieces[piece])], load.at[sem])

    barrier = pltpu.get_barrier_semaphore()

    def greet(to):
        pl.semaphore_signal(barrier, inc=1, device_id=(to,), device_id_type=MESH)

    greet(partner)

    @pl.when(owns)
    def _():
        for j in range(1, 16):
            o = (zc + j) % 16
            greet(device(x, y, o // 2, o % 2))

    @pl.when(owns_8)
    def _():
        for h in range(2):
            for j in range(8):
                greet(device(half + h, j, z, c))

    def siblings(n):
        node = y // n
        first = (node + 1 - 2 * (node % 2)) * n
        return [device(x, first + j, z, c) for j in range(n)]

    @pl.when(at(1))
    def _():
        for to in siblings(1) + siblings(2):
            greet(to)

    @pl.when(at(2))
    def _():
        for j in range(8):
            greet(device(beside, j, z, c))

    @pl.when(at(3))
    def _():
        for to in siblings(4):
            greet(to)

    probes_in.wait()
    await_rows(0, 0)
    signs[...] = (2 * probes[...] - 1).astype(BF16)

    def coefs(bases, first, count):
        return nt(signs[...], bases[pl.ds(first, count), :])

    def lanes(part, k):
        return part[:, k * 128 : (k + 1) * 128]

    def hand_over(first, part, count, i):
        for k in range(count):
            give[first + k] = lanes(part, k)
        rows = pl.ds(first, count)
        send(give.at[rows], take.at[rows], sent, rx.at[i], partner)

    other_8 = coefs(other, TOP8 + 256, 256)

    for place, count in enumerate((20, 23, 12, 8)):
        @pl.when(at(place))
        def _():
            pl.semaphore_wait(barrier, count)

    @pl.when(jnp.logical_not(owns))
    def _():
        pl.semaphore_wait(barrier, 5)

    hand_over(2, other_8, 2, 0)
    hand_over(0, coefs(other, TOP8, 256), 2, 3)
    await_rows(0, 1)
    await_rows(1, 1)
    hand_over(4, coefs(other, TOP67, 512), 4, 1)

    def to_owner(place, rows, recv_sem, split=0):
        @pl.when(jnp.logical_not(at(place)))
        def _():
            send(
                snd.at[place, rows], got.at[z, rows, c], sent, rs.at[recv_sem + split * (1 - c)],
                device(x, y, place, 1),
            )

        @pl.when(at(place))
        def _():
            got[place, rows, 1] = snd[place, rows]

    for place, i in ((1, 0), (0, 3)):
        own_8 = coefs(own, TOP8 + 256 * place, 256)
        wait(take.at[pl.ds(2 * place, 2)], rx.at[i])
        for k in range(2):
            snd[place, k] = (lanes(own_8, k) + take[2 * place + k]).astype(BF16)
        to_owner(place, pl.ds(0, 2), 0, 10)

    await_rows(1, 2)
    own_67 = coefs(own, TOP67, 512)

    wait(take.at[pl.ds(4, 4)], rx.at[1])
    for k in range(4):
        snd[3 - k // 2, k % 2] = (lanes(own_67, k) + take[4 + k]).astype(BF16)
    for place in (2, 3):
        to_owner(place, pl.ds(0, 2), 0, 10)

    coords_in.wait()
    await_rows(2, 3)
    await_rows(2, 3)
    spots = coords[...].astype(F32) / cell_units
    for leaf in range(2):
        cols = pl.ds(leaf * LEAF, LEAF)
        across = pl.ds((1 - leaf) * LEAF, LEAF)
        near = nn(signs[:, cols], matern(spots, leaf))
        coef_f = nt(signs[:, across], v[pl.ds(0, 64), across]).astype(BF16)
        coef_t = nt(signs[:, across], u[pl.ds(0, 64), across]).astype(BF16)
        out_ref[:16, cols] = near + nn(coef_f, u[pl.ds(0, 64), cols])
        out_ref[16:, cols] = near + nn(coef_t, v[pl.ds(0, 64), cols])

    other_low = coefs(other, 64, 512)
    hand_over(8, other_low, 4, 2)
    own_low = coefs(own, 64, 512)
    f_0 = jnp.where(core0, own_low[:, :64], other_low[:, :64])
    t_0 = jnp.where(core0, other_low[:, :64], own_low[:, :64])
    low0[...] = jnp.concatenate([f_0, t_0], axis=1).astype(BF16)
    send(low0, fin0, sent, rs.at[2], partner)
    wait(take.at[pl.ds(8, 4)], rx.at[2])
    for k, (place, row) in enumerate(((0, 2), (1, 2), (1, 3), (1, 4))):
        snd[place, row] = (lanes(own_low, k) + take[8 + k]).astype(BF16)
    to_owner(1, pl.ds(3, 2), 1)
    to_owner(1, pl.ds(2, 1), 9)
    to_owner(0, pl.ds(2, 1), 1)

    def total(parts):
        return sum(part.astype(F32) for part in parts)

    def add_up(into, row, parts):
        for kind in range(2):
            into[row, kind] = total(part[kind] for part in parts).astype(BF16)

    for kind, count, sem in ((1, 14, 0), (0, 16, 10)):
        @pl.when(owns)
        def _():
            wait(chunks(count), rs.at[sem])
            for a in range(2):
                mine[a, kind] = total(got[k, a, kind] for k in range(8)).astype(BF16)

        @pl.when(owns_8)
        def _():
            rows = pl.ds(0, 2)
            for j in (0, 1, 7, 2, 6, 3, 5, 4):
                for h in range(2):
                    to = device(half + h, j, z, c)
                    slot = q8.at[(x % 2) * 8 + y, rows, kind]
                    send(mine.at[rows, kind], slot, sent, rs.at[3], to)

    @pl.when(at(2))
    def _():
        for j in (0, 1, 7, 2, 6, 3, 5, 4):
            send(mine.at[pl.ds(0, 2)], q7.at[y], sent, rs.at[3], device(beside, j, z, c))

    @pl.when(at(3))
    def _():
        for to in siblings(4):
            send(mine.at[pl.ds(0, 2)], q6.at[y % 4], sent, rs.at[3], to)

    def hand_out_low(own_place, source, recv_sem):
        for place in (0, 1, 2, 3, 4, 5, 6, 7):
            if place == own_place:
                fin[own_place, 2] = source(place)[...]
                send(source(place), fin.at[own_place, 2], sent, rs.at[recv_sem], partner)
            else:
                for core in (1, 0):
                    to = device(x, y, place, core)
                    send(source(place), fin.at[own_place, 2], sent, rs.at[recv_sem], to)

    @pl.when(at(0))
    def _():
        wait(chunks(15), rs.at[1])
        hand_out_low(0, lambda place: got.at[place ^ 1, 2], 2)

    @pl.when(at(1))
    def _():
        wait(chunks(30), rs.at[1])
        wait(chunks(15), rs.at[9])
        for a in (3, 4):
            add_up(mine, a, [got.at[k, a] for k in range(8)])
        for to in siblings(1):
            send(mine.at[3], q45.at[0], sent, rs.at[4], to)
        for to in siblings(2):
            send(mine.at[4], q45.at[1 + y % 2], sent, rs.at[4], to)
        lane = lax.broadcasted_iota(jnp.int32, (16, 128), 1)
        for kind in range(2):
            pairs = [total(got[2 * k + i, 2, kind] for i in range(2)) for k in range(4)]
            quads = [pairs[0] + pairs[1], pairs[2] + pairs[3]]
            for k in range(4):
                low_out[k, kind] = jnp.where(lane < 64, pairs[k ^ 1], quads[1 - k // 2]).astype(BF16)
        hand_out_low(1, lambda place: low_out.at[place // 2], 2)

    def hand_out(own_place, rows, recv_sem, places):
        src = fin.at[own_place, rows]
        for place in places:
            if place == own_place:
                send(src, src, sent, rs.at[recv_sem], partner)
            else:
                for core in (1, 0):
                    to = device(x, y, place, core)
                    send(src, src, sent, rs.at[recv_sem], to)

    @pl.when(at(1))
    def _():
        wait(q45, rs.at[4])
        fin[1, 3] = q45[0]
        add_up(fin.at[1], 4, [q45.at[1 + k] for k in range(2)])
        hand_out(1, pl.ds(3, 2), 5, range(8))

    @pl.when(at(2))
    def _():
        wait(q7, rs.at[3])
        for a in range(2):
            add_up(fin.at[2], a, [q7.at[k, a] for k in range(8)])
        hand_out(2, pl.ds(0, 2), 6, range(6))

    @pl.when(at(3))
    def _():
        wait(q6, rs.at[3])
        for a in range(2):
            add_up(fin.at[3], a, [q6.at[k, a] for k in range(4)])
        hand_out(3, pl.ds(0, 2), 6, range(7))

    for own_place in range(2):
        @pl.when(at(own_place))
        def _():
            wait(q8, rs.at[3])
            for a in range(2):
                add_up(fin.at[own_place], a, [q8.at[k, a] for k in range(16)])
            hand_out(own_place, pl.ds(0, 2), 7 + own_place, range(8 - 3 * own_place))

    def await_chunks(most, least, sem, is_own):
        if least:
            @pl.when(is_own)
            def _():
                wait(chunks(least), rs.at[sem])

        @pl.when(jnp.logical_not(is_own))
        def _():
            wait(chunks(most), rs.at[sem])

    await_chunks(5, 3, 2, owns_8)
    low_f = jnp.concatenate([fin0[:, :64], fin[0, 2, 0][:, 64:], fin[1, 2, 0]], axis=1)
    low_t = jnp.concatenate([fin0[:, 64:], fin[0, 2, 1][:, 64:], fin[1, 2, 1]], axis=1)
    out_ref[:16, :] += nn(low_f, u[pl.ds(64, 256), :])
    out_ref[16:, :] += nn(low_t, v[pl.ds(64, 256), :])

    await_chunks(4, 0, 5, at(1))

    def add(places, first):
        count = 128 * len(places)
        for kind, bases in ((0, u), (1, v)):
            coefs_here = jnp.concatenate([fin[place, row, kind] for place, row in places], axis=1)
            out_ref[kind * 16 : kind * 16 + 16, :] += nn(coefs_here, bases[pl.ds(first, count), :])

    add([(1, 3), (1, 4)], MID)

    await_chunks(8, 4, 6, owns_67)

    @pl.when(at(1))
    def _():
        hand_out(1, pl.ds(0, 2), 8, (5, 6, 7))

    add([(3, 0), (3, 1), (2, 0), (2, 1)], TOP67)

    for place in range(2):
        await_chunks(4, 0, 7 + place, at(place))
        add([(place, 0), (place, 1)], TOP8 + 256 * place)

    @pl.when(at(2))
    def _():
        hand_out(2, pl.ds(0, 2), 6, (6, 7))

    @pl.when(at(3))
    def _():
        hand_out(3, pl.ds(0, 2), 6, (7,))

    wait(give, sent)

    def left(*sizes):
        for n in sizes:
            wait(chunks(n), sent)

    @pl.when(jnp.logical_not(owns))
    def _():
        left(13)

    @pl.when(at(0))
    def _():
        left(10, 64, 30, 60)

    @pl.when(at(1))
    def _():
        left(8, 64, 6, 30, 60, 60)

    @pl.when(at(2))
    def _():
        left(11, 32, 60)

    @pl.when(at(3))
    def _():
        left(11, 16, 60)


def shards(coords, probes, u_bases, v_bases):
    tile = (16, 128)
    operands = [
        pltpu.with_memory_space_constraint(a, pltpu.HBM) for a in (coords, probes, u_bases, v_bases)
    ]
    both = pl.pallas_call(
        kernel,
        out_shape=jax.ShapeDtypeStruct((32, POINTS_HERE), F32),
        in_specs=[pl.BlockSpec(memory_space=pl.ANY)] * 4,
        out_specs=pl.BlockSpec(memory_space=pltpu.VMEM),
        scratch_shapes=[
            pltpu.VMEM((2, POINTS_HERE), jnp.int32),
            pltpu.VMEM((16, POINTS_HERE), jnp.int32),
            pltpu.VMEM((16, POINTS_HERE), BF16),
            pltpu.VMEM((2, RANKS, POINTS_HERE), BF16),
            pltpu.VMEM((12,) + tile, F32),
            pltpu.VMEM((12,) + tile, F32),
            pltpu.VMEM((4, 5) + tile, BF16),
            pltpu.VMEM(tile, BF16),
            pltpu.VMEM((8, 5, 2) + tile, BF16),
            pltpu.VMEM((5, 2) + tile, BF16),
            pltpu.VMEM((16, 2, 2) + tile, BF16),
            pltpu.VMEM((8, 2, 2) + tile, BF16),
            pltpu.VMEM((4, 2, 2) + tile, BF16),
            pltpu.VMEM((3, 2) + tile, BF16),
            pltpu.VMEM((4, 2) + tile, BF16),
            pltpu.VMEM((4, 5, 2) + tile, BF16),
            pltpu.VMEM(tile, BF16),
            pltpu.SemaphoreType.DMA((4,)),
            pltpu.SemaphoreType.DMA,
            pltpu.SemaphoreType.DMA((4,)),
            pltpu.SemaphoreType.DMA((11,)),
        ],
        compiler_params=pltpu.CompilerParams(
            collective_id=0, has_side_effects=True, vmem_limit_bytes=VMEM_BYTES
        ),
    )(*operands)
    return both[:16], both[16:]


def solution(mesh):
    return jax.shard_map(
        shards,
        mesh=mesh,
        in_specs=(P(None, "pts"), P(None, "pts"), P(None, "pts"), P(None, "pts")),
        out_specs=(P(None, "pts"), P(None, "pts")),
        check_vma=False,
    )
```
